32 devices in a mesh: group: 2 (over x), tile: 16 (over z, y, core).
Axes of the slice: x: 2, y: 2, z: 4, core: 2. Of those that a mesh axis runs over, the one named last changes fastest.
Arguments:
- facies: int32 [128, 128, 256], P('group', 'tile'), may hold values from 0 to 7
- perm_table: float32 [8], replicated, may hold values from 0.05 to 10
- source: float32 [128, 128, 256], P('group', 'tile'), may hold values from -6 to 6
Outputs:
- head: float32 [128, 128, 256], P('group', 'tile')
The draws below stay inside these ranges and needn't reach their ends.
All inputs are finite; a program needn't handle non-finite values.
Results may differ from the reference program's by a relative error of at most 0.0003.
Values sent between devices are 32-bit elements; how exact they have to be, the bound alone decides.
A program may use at most 64 MiB of HBM per device.

```python
import math
import jax
import jax.numpy as jnp
from jax import lax

CX = 64
CY = 8
CZ = 256
NF = 8
COARSE_ITERS = 3
NX = 128
NY = 128
N_GROUP = 2
N_TILE = 16


def draw_facies(key, part):
    key_plane, key_low, key_high = jax.random.split(jax.random.fold_in(key, 11), 3)
    plane_kind = jax.random.randint(key_plane, (NX, 1, 1), 0, 3)
    low_kind = jax.random.randint(key_low, (NX, NY, CZ), 0, 2)
    high_kind = jax.random.randint(key_high, (NX, NY, CZ), 2, NF)
    return jnp.where(plane_kind == 0, high_kind, low_kind).astype(jnp.int32)


def draw_perm_table(key, part):
    key_low, key_high = jax.random.split(jax.random.fold_in(key, 7))
    u_low = jax.random.uniform(key_low, (NF,), jnp.float32)
    u_high = jax.random.uniform(key_high, (NF,), jnp.float32)
    low_perm = 0.05 * jnp.exp(u_low * math.log(2.0))
    high_perm = 2.0 * jnp.exp(u_high * math.log(5.0))
    return jnp.where(jnp.arange(NF) < 2, low_perm, high_perm).astype(jnp.float32)


def block_levels(rng, dims, cuts, least, largest):
    gain = 1.0
    for position, parts in cuts:
        draws = jax.random.uniform(jax.random.fold_in(jax.random.fold_in(rng, 6), position), (parts,), jnp.float32, least / len(cuts), largest / len(cuts))
        gain = gain * jnp.repeat(jnp.exp(draws), dims[position] // parts).reshape((-1,) + (1,) * (len(dims) - 1 - position))
    return gain


def normal_values(rng, dims, scale, bound, pieces=(), dtype=jnp.bfloat16):
    loudness = block_levels(rng, dims, pieces, -0.22, 0.18) if pieces else 1.0
    result = jax.random.normal(rng, dims, jnp.float32) * scale * loudness
    return jnp.minimum(jnp.maximum(result, -bound), bound).astype(dtype)


def setup_inputs(seed: int = 0) -> dict:
    arg_keys = jax.random.split(jax.random.key(seed), 4)
    facies = draw_facies(jax.random.fold_in(arg_keys[3], 71), 0)
    perm_table = draw_perm_table(jax.random.fold_in(arg_keys[3], 71), 0)
    source = normal_values(arg_keys[2], (NX, NY, CZ), 1.0, 6.0, ((0, 2), (1, 16)), jnp.float32)
    return {"facies": facies, "perm_table": perm_table, "source": source}


relax_weight = 0.8

def harmonic(left_perm, right_perm):
    pair_sum = left_perm + right_perm
    positive = pair_sum > 0.0
    return jnp.where(positive, 2.0 * left_perm * right_perm / jnp.where(positive, pair_sum, 1.0), 0.0)

def operator(head_ext, perm_ext, storage):
    perm_mid = perm_ext[1:-1, 1:-1]
    head_mid = head_ext[1:-1, 1:-1]
    flux_sum = storage * head_mid
    diagonal = storage + jnp.zeros_like(head_mid)
    pairs = [(perm_ext[2:, 1:-1], head_ext[2:, 1:-1]), (perm_ext[:-2, 1:-1], head_ext[:-2, 1:-1]), (perm_ext[1:-1, 2:], head_ext[1:-1, 2:]), (perm_ext[1:-1, :-2], head_ext[1:-1, :-2])]
    perm_z = jnp.pad(perm_mid, ((0, 0), (0, 0), (1, 1)))
    head_z = jnp.pad(head_mid, ((0, 0), (0, 0), (1, 1)))
    pairs = pairs + [(perm_z[:, :, 2:], head_z[:, :, 2:]), (perm_z[:, :, :-2], head_z[:, :, :-2])]
    for perm_nb, head_nb in pairs:
        trans = harmonic(perm_mid, perm_nb)
        flux_sum = flux_sum + trans * (head_mid - head_nb)
        diagonal = diagonal + trans
    return (flux_sum, diagonal)

def sweep(head_ext, perm_ext, rhs_mid, storage):
    flux_sum, diagonal = operator(head_ext, perm_ext, storage)
    return head_ext[1:-1, 1:-1] + relax_weight * (rhs_mid - flux_sum) / diagonal

def coarse_solve(coarse_rhs, link_x, link_y, store_brick):
    zero_row = jnp.zeros_like(coarse_rhs[:1])
    zero_col = jnp.zeros_like(coarse_rhs[:, :1])
    link_x_prev = jnp.concatenate([zero_row, link_x[:-1]], axis=0)
    link_y_prev = jnp.concatenate([zero_col, link_y[:, :-1]], axis=1)
    diagonal = store_brick + link_x + link_x_prev + link_y + link_y_prev
    lower = -link_y_prev
    upper = -link_y
    correction = jnp.zeros_like(coarse_rhs)
    for sweep_no in range(COARSE_ITERS):
        before = jnp.concatenate([zero_row, correction[:-1]], axis=0)
        after = jnp.concatenate([correction[1:], zero_row], axis=0)
        rhs_now = coarse_rhs + link_x_prev * before + link_x * after
        correction = lax.linalg.tridiagonal_solve(lower, diagonal, upper, rhs_now[..., None])[..., 0]
    return correction

def pad_plane(field):
    return jnp.pad(field, ((1, 1), (1, 1), (0, 0)))

def reference(facies, perm_table, source):
    storage = 0.01 / CY
    perm = perm_table[facies]
    perm_pad = pad_plane(perm)
    head_zero = jnp.zeros(perm_pad.shape, jnp.float32)
    head_one = sweep(head_zero, perm_pad, source, storage)
    head_two = sweep(pad_plane(head_one), perm_pad, source, storage)
    flux_sum, unused = operator(pad_plane(head_two), perm_pad, storage)
    resid = source - flux_sum
    coarse_rhs = resid.reshape(N_GROUP, CX, N_TILE, CY, CZ).sum(axis=(1, 3, 4))
    last_x = perm[CX - 1::CX]
    next_x = jnp.concatenate([perm[CX::CX], jnp.zeros_like(perm[:1])], axis=0)
    link_x = harmonic(last_x, next_x).sum(axis=2).reshape(N_GROUP, N_TILE, CY).sum(axis=2)
    last_y = perm[:, CY - 1::CY]
    next_y = jnp.concatenate([perm[:, CY::CY], jnp.zeros_like(perm[:, :1])], axis=1)
    link_y = harmonic(last_y, next_y).sum(axis=2).reshape(N_GROUP, CX, N_TILE).sum(axis=1)
    correction = coarse_solve(coarse_rhs, link_x, link_y, storage * CX * CY * CZ)
    spread = jnp.repeat(jnp.repeat(correction, CX, axis=0), CY, axis=1)
    head_three = head_two + spread[:, :, None]
    head_four = sweep(pad_plane(head_three), perm_pad, source, storage)
    return sweep(pad_plane(head_four), perm_pad, source, storage)
```

```python
import functools

import jax
import jax.numpy as jnp
from jax import lax
from jax.experimental import pallas as pl
from jax.experimental.pallas import tpu as pltpu
from jax.sharding import PartitionSpec as P

COARSE_ITERS = 3
RELAX = 0.8
MESH = pl.DeviceIdType.MESH
F32 = jnp.float32

PW = 3
SW = 2
XH = 8
SIDES = [(0, 1), (0, -1), (1, 0), (-1, 0), (1, 1), (1, -1), (-1, 1), (-1, -1)]


def harmonic(p, q):
    return 2.0 * p * q / jnp.maximum(p + q, 1e-30)


def kernel(groups, tiles, facies, table, source, out, fac, perm, src, tx, ty, tz, wt, h1, h2, h4, res,
           mine, gath, in_sem, out_sem, send_sem, recv_sem, cs_sem, cr_sem):
    cx, cy, cz = source.shape
    nf = table.shape[0]
    n = groups * tiles
    g = lax.axis_index("group")
    t = lax.axis_index("tile")
    me = g * tiles + t
    ex = cx + 2 * XH
    y0, y1 = PW, PW + cy
    storage = 0.01 / cy

    barrier = pltpu.get_barrier_semaphore()

    def greet(k, carry):
        other = lax.rem(me + k, n)
        pl.semaphore_signal(barrier, inc=1, device_id=(other // tiles, lax.rem(other, tiles)), device_id_type=MESH)
        return carry

    lax.fori_loop(1, n, greet, 0)

    loads_s = [pltpu.make_async_copy(source.at[:, y, :], src.at[y0 + y, pl.ds(XH, cx), :], in_sem.at[y]) for y in range(cy)]
    loads_f = [pltpu.make_async_copy(facies.at[:, y, :], fac.at[y], in_sem.at[cy + y]) for y in range(cy)]
    for c in loads_f + loads_s:
        c.start()

    def exists(dg, dt):
        ok = None
        for pos, d, count in ((g, dg, groups), (t, dt, tiles)):
            if d:
                one = pos < count - 1 if d > 0 else pos > 0
                ok = one if ok is None else jnp.logical_and(ok, one)
        return ok

    def span(dg, dt, w):
        ys, yd, yn = {0: (y0, y0, cy), 1: (y1 - w, y0 - w, w), -1: (y0, y1, w)}[dt]
        xs, xd, xn = {0: (XH, XH, cx), 1: (cx, 0, XH), -1: (XH, XH + cx, XH)}[dg]
        return (pl.ds(ys, yn), pl.ds(xs, xn)), (pl.ds(yd, yn), pl.ds(xd, xn))

    def halo(buf, w, slot, sides):
        copies = []
        for k, (dg, dt) in enumerate(sides):
            a, b = span(dg, dt, w)
            copies.append(pltpu.make_async_remote_copy(
                src_ref=buf.at[a], dst_ref=buf.at[b], send_sem=send_sem.at[slot, k], recv_sem=recv_sem.at[slot, k],
                device_id=(g + dg, t + dt), device_id_type=MESH))
        return copies

    def blank(buf, w, sides):
        for dg, dt in sides:
            _, b = span(dg, dt, w)

            @pl.when(jnp.logical_not(exists(-dg, -dt)))
            def _():
                buf[b] = jnp.zeros((b[0].size, b[1].size, cz), F32)

    def begin(copies, sides):
        for c, (dg, dt) in zip(copies, sides):
            pl.when(exists(dg, dt))(c.start)

    def landed(copies, sides):
        for c, (dg, dt) in zip(copies, sides):
            pl.when(exists(-dg, -dt))(c.wait_recv)

    def left(copies, sides):
        for c, (dg, dt) in zip(copies, sides):
            pl.when(exists(dg, dt))(c.wait_send)

    blank(perm, PW, SIDES)
    blank(src, SW, SIDES)
    blank(h4, 1, SIDES[:4])
    for c in loads_f:
        c.wait()

    def paint(y, carry):
        f = fac[y]
        p = jnp.zeros((cx, cz), F32)
        for k in range(nf):
            p = jnp.where(f == k, table[k], p)
        perm[y0 + y, pl.ds(XH, cx), :] = p
        return carry

    lax.fori_loop(0, cy, paint, 0)
    for c in loads_s:
        c.wait()
    pl.semaphore_wait(barrier, n - 1)
    perm_out = halo(perm, PW, 0, SIDES)
    src_out = halo(src, SW, 1, SIDES)
    begin(perm_out, SIDES)
    begin(src_out, SIDES)
    landed(perm_out, SIDES)
    landed(src_out, SIDES)

    def xp(v):
        return pltpu.roll(v, ex - 1, 0)

    def xm(v):
        return pltpu.roll(v, 1, 0)

    def zp(v):
        return pltpu.roll(v, cz - 1, 1)

    def zm(v):
        return pltpu.roll(v, 1, 1)

    last_z = lax.broadcasted_iota(jnp.int32, (ex, cz), 1) == cz - 1

    ty[0] = harmonic(perm[0], perm[1])

    def faces(y, carry):
        p = perm[y]
        fx = harmonic(p, xp(p))
        fz = jnp.where(last_z, 0.0, harmonic(p, zp(p)))
        fy = harmonic(p, perm[y + 1])
        tx[y] = fx
        tz[y] = fz
        ty[y] = fy
        diag = storage + fx + xm(fx) + fz + zm(fz) + fy + ty[y - 1]
        w = RELAX / diag
        wt[y] = w
        h1[y] = w * src[y]
        return carry

    lax.fori_loop(y0 - 2, y1 + 2, faces, 0)

    def sweep(v_ref, y):
        v = v_ref[y]
        fx = tx[y] * (v - xp(v))
        fz = tz[y] * (v - zp(v))
        flux = storage * v + (fx - xm(fx)) + (fz - zm(fz))
        flux = flux + ty[y] * (v - v_ref[y + 1]) + ty[y - 1] * (v - v_ref[y - 1])
        return v + (src[y] - flux) * wt[y]

    def second(y, carry):
        h2[y] = sweep(h1, y)
        return carry

    lax.fori_loop(y0 - 1, y1 + 1, second, 0)

    own = pl.ds(XH, cx)

    def gather_sum(y, acc):
        v = h2[y]
        fx = tx[y] * (v - xp(v))
        inner = src[y, own, :] - storage * h2[y, own, :]
        acc = acc + jnp.sum(inner.reshape(cx // 8, 8, cz), axis=0)
        hi = fx[XH + cx - 8:XH + cx]
        lo = fx[XH - 8:XH]
        row = lax.broadcasted_iota(jnp.int32, (8, cz), 0) == 7
        return acc + jnp.where(row, lo - hi, 0.0)

    acc = lax.fori_loop(y0, y1, gather_sum, jnp.zeros((8, cz), F32))
    edge = ty[y1 - 1, own, :] * (h2[y1 - 1, own, :] - h2[y1, own, :]) + ty[y0 - 1, own, :] * (h2[y0, own, :] - h2[y0 - 1, own, :])
    acc = acc - jnp.sum(edge.reshape(cx // 8, 8, cz), axis=0)
    rhs = jnp.sum(jnp.sum(acc, axis=0, keepdims=True), axis=1, keepdims=True)
    link_x = jnp.sum(jnp.sum(tx[pl.ds(y0, cy), pl.ds(XH + cx - 8, 8), :][:, 7, :], axis=0, keepdims=True), axis=1, keepdims=True)
    link_y = jnp.sum(jnp.sum(ty[y1 - 1, own, :], axis=0, keepdims=True), axis=1, keepdims=True)
    lane = lax.broadcasted_iota(jnp.int32, (1, 128), 1)
    packed = jnp.where(lane == g, rhs, jnp.where(lane == g + 32, link_x, jnp.where(lane == g + 64, link_y, 0.0)))
    mine[...] = packed
    gath[me] = packed

    def to(other):
        return pltpu.make_async_remote_copy(
            src_ref=mine, dst_ref=gath.at[me], send_sem=cs_sem, recv_sem=cr_sem,
            device_id=(other // tiles, lax.rem(other, tiles)), device_id_type=MESH)

    def tell(k, carry):
        to(lax.rem(me + k, n)).start()
        return carry

    lax.fori_loop(1, n, tell, 0)
    rest = gath.at[pl.ds(0, n - 1)]
    pltpu.make_async_copy(rest, rest, cr_sem).wait()

    lanes = lax.broadcasted_iota(jnp.int32, (tiles, 128), 1)
    whole = jnp.sum(gath[...].reshape(groups, tiles, 128), axis=0)
    c_rhs = jnp.where(lanes < groups, whole, 0.0)
    c_lx = jnp.where(lanes < groups, pltpu.roll(whole, 96, 1), 0.0)
    c_ly = jnp.where(lanes < groups, pltpu.roll(whole, 64, 1), 0.0)

    def before(v, s):
        return pltpu.roll(v, s, 0)

    def after(v, s):
        return pltpu.roll(v, tiles - s, 0)

    lx_prev = pltpu.roll(c_lx, 1, 1)
    ly_prev = before(c_ly, 1)
    diag = storage * cx * cy * cz + c_lx + lx_prev + c_ly + ly_prev
    lower, upper = -ly_prev, -c_ly
    steps = []
    stride = 1
    while stride < tiles:
        alpha = -lower / before(diag, stride)
        gamma = -upper / after(diag, stride)
        steps.append((stride, alpha, gamma))
        diag = diag + alpha * before(upper, stride) + gamma * after(lower, stride)
        lower, upper = alpha * before(lower, stride), gamma * after(upper, stride)
        stride *= 2
    inv = 1.0 / diag
    corr = jnp.zeros((tiles, 128), F32)
    for _ in range(COARSE_ITERS):
        r = c_rhs + lx_prev * pltpu.roll(corr, 1, 1) + c_lx * pltpu.roll(corr, 127, 1)
        for stride, alpha, gamma in steps:
            r = r + alpha * before(r, stride) + gamma * after(r, stride)
        corr = r * inv

    row_t = lax.broadcasted_iota(jnp.int32, (tiles, 128), 0)

    def pick(dg, dt):
        hit = jnp.logical_and(row_t == t + dt, lanes == g + dg)
        one = jnp.sum(jnp.where(hit, corr, 0.0), axis=0, keepdims=True)
        return jnp.broadcast_to(jnp.sum(one, axis=1, keepdims=True), (1, cz))

    c_own, c_low, c_high = pick(0, 0), pick(0, -1), pick(0, 1)
    c_left, c_right = pick(-1, 0), pick(1, 0)
    xrow = lax.broadcasted_iota(jnp.int32, (ex, cz), 0)
    c_mid = jnp.where(xrow < XH, c_left, jnp.where(xrow < XH + cx, c_own, c_right))
    h2[y0 - 1] = h2[y0 - 1] + c_low
    h2[y1] = h2[y1] + c_high

    def shift(y, carry):
        h2[y] = h2[y] + c_mid
        return carry

    lax.fori_loop(y0, y1, shift, 0)

    def fourth(y, carry):
        h4[y, own, :] = sweep(h2, y)[XH:XH + cx]
        return carry

    lax.fori_loop(y0, y1, fourth, 0)
    four = SIDES[:4]
    h4_out = halo(h4, 1, 2, four)
    begin(h4_out, four)
    landed(h4_out, four)

    h4[y0 - 1, pl.ds(0, XH), :] = jnp.zeros((XH, cz), F32)
    h4[y0 - 1, pl.ds(XH + cx, XH), :] = jnp.zeros((XH, cz), F32)
    h4[y1, pl.ds(0, XH), :] = jnp.zeros((XH, cz), F32)
    h4[y1, pl.ds(XH + cx, XH), :] = jnp.zeros((XH, cz), F32)

    def last(y, carry):
        res[y - y0] = sweep(h4, y)[XH:XH + cx]
        return carry

    lax.fori_loop(y0, y1, last, 0)
    stores = [pltpu.make_async_copy(res.at[y], out.at[:, y, :], out_sem.at[y]) for y in range(cy)]
    for c in stores:
        c.start()
    left(perm_out, SIDES)
    left(src_out, SIDES)
    left(h4_out, four)
    pltpu.make_async_copy(rest, rest, cs_sem).wait()
    for c in stores:
        c.wait()


def solution(mesh):
    groups, tiles = mesh.shape["group"], mesh.shape["tile"]

    def on_device(facies, table, source):
        cx, cy, cz = source.shape
        ext = pltpu.VMEM((cy + 2 * PW, cx + 2 * XH, cz), F32)
        n = groups * tiles
        return pl.pallas_call(
            functools.partial(kernel, groups, tiles),
            out_shape=jax.ShapeDtypeStruct(source.shape, F32),
            in_specs=[pl.BlockSpec(memory_space=pl.ANY), pl.BlockSpec(memory_space=pltpu.SMEM), pl.BlockSpec(memory_space=pl.ANY)],
            out_specs=pl.BlockSpec(memory_space=pl.ANY),
            scratch_shapes=[
                pltpu.VMEM((cy, cx, cz), jnp.int32),
                ext, ext, ext, ext, ext, ext, ext, ext, ext,
                pltpu.VMEM((cy, cx, cz), F32),
                pltpu.VMEM((1, 128), F32),
                pltpu.VMEM((n, 1, 128), F32),
                pltpu.SemaphoreType.DMA((2 * cy,)),
                pltpu.SemaphoreType.DMA((cy,)),
                pltpu.SemaphoreType.DMA((3, 8)),
                pltpu.SemaphoreType.DMA((3, 8)),
                pltpu.SemaphoreType.DMA,
                pltpu.SemaphoreType.DMA,
            ],
            compiler_params=pltpu.CompilerParams(
                collective_id=0, has_side_effects=True, vmem_limit_bytes=48 * 1024 * 1024),
        )(facies, table, source)

    placed = (P("group", "tile", None), P(), P("group", "tile", None))
    return jax.shard_map(on_device, mesh=mesh, in_specs=placed, out_specs=P("group", "tile", None), check_vma=False)
```

```python
import functools

import jax
import jax.numpy as jnp
from jax import lax
from jax.experimental import pallas as pl
from jax.experimental.pallas import tpu as pltpu
from jax.sharding import PartitionSpec as P

COARSE_ITERS = 3
RELAX = 0.8
MESH = pl.DeviceIdType.MESH
F32 = jnp.float32

PW = 3
SW = 2
XH = 8
SIDES = [(0, 1), (0, -1), (1, 0), (-1, 0), (1, 1), (1, -1), (-1, 1), (-1, -1)]


FAR = 1e36


def recip(x):
    y = pl.reciprocal(x, approx=True)
    return y * (2.0 - x * y)


def kernel(groups, tiles, facies, table, source, out, fac, half, src, tx, ty, tz, wt, h1, h2, h4, s2, res,
           mine, gath, in_sem, out_sem, send_sem, recv_sem, cs_sem, cr_sem):
    cx, cy, cz = source.shape
    nf = table.shape[0]
    n = groups * tiles
    g = lax.axis_index("group")
    t = lax.axis_index("tile")
    me = g * tiles + t
    ex = cx + 2 * XH
    y0, y1 = PW, PW + cy
    storage = 0.01 / cy

    barrier = pltpu.get_barrier_semaphore()

    def greet(k, carry):
        other = lax.rem(me + k, n)
        pl.semaphore_signal(barrier, inc=1, device_id=(other // tiles, lax.rem(other, tiles)), device_id_type=MESH)
        return carry

    lax.fori_loop(1, n, greet, 0)

    loads_s = [pltpu.make_async_copy(source.at[:, y, :], src.at[y0 + y, pl.ds(XH, cx), :], in_sem.at[y]) for y in range(cy)]
    loads_f = [pltpu.make_async_copy(facies.at[:, y, :], fac.at[y], in_sem.at[cy + y]) for y in range(cy)]
    for c in loads_f + loads_s:
        c.start()

    def exists(dg, dt):
        ok = None
        for pos, d, count in ((g, dg, groups), (t, dt, tiles)):
            if d:
                one = pos < count - 1 if d > 0 else pos > 0
                ok = one if ok is None else jnp.logical_and(ok, one)
        return ok

    def span(dg, dt, w):
        ys, yd, yn = {0: (y0, y0, cy), 1: (y1 - w, y0 - w, w), -1: (y0, y1, w)}[dt]
        xs, xd, xn = {0: (XH, XH, cx), 1: (cx, 0, XH), -1: (XH, XH + cx, XH)}[dg]
        return (pl.ds(ys, yn), pl.ds(xs, xn)), (pl.ds(yd, yn), pl.ds(xd, xn))

    def halo(buf, w, slot, sides):
        copies = []
        for k, (dg, dt) in enumerate(sides):
            a, b = span(dg, dt, w)
            copies.append(pltpu.make_async_remote_copy(
                src_ref=buf.at[a], dst_ref=buf.at[b], send_sem=send_sem.at[slot, k], recv_sem=recv_sem.at[slot, k],
                device_id=(g + dg, t + dt), device_id_type=MESH))
        return copies

    def blank(buf, w, sides, value):
        for dg, dt in sides:
            _, b = span(dg, dt, w)

            @pl.when(jnp.logical_not(exists(-dg, -dt)))
            def _():
                buf[b] = jnp.full((b[0].size, b[1].size, cz), value, F32)

    def begin(copies, sides):
        for c, (dg, dt) in zip(copies, sides):
            pl.when(exists(dg, dt))(c.start)

    def landed(copies, sides):
        for c, (dg, dt) in zip(copies, sides):
            pl.when(exists(-dg, -dt))(c.wait_recv)

    def left(copies, sides):
        for c, (dg, dt) in zip(copies, sides):
            pl.when(exists(dg, dt))(c.wait_send)

    blank(half, PW, SIDES, FAR)
    blank(src, SW, SIDES, 0.0)
    blank(s2, 1, SIDES[:4], 0.0)
    kinds = [0.5 / jnp.full((1, cz), table[k], F32) for k in range(nf)]
    for c in loads_f:
        c.wait()

    def paint(y, carry):
        f = fac[y]
        p = jnp.broadcast_to(kinds[0], (cx, cz))
        for k in range(1, nf):
            p = jnp.where(f == k, kinds[k], p)
        half[y0 + y, pl.ds(XH, cx), :] = p
        return carry

    lax.fori_loop(0, cy, paint, 0)
    pl.semaphore_wait(barrier, n - 1)
    half_out = halo(half, PW, 0, SIDES)
    src_out = halo(src, SW, 1, SIDES)
    begin(half_out, SIDES)
    for c in loads_s:
        c.wait()
    begin(src_out, SIDES)

    def xp(v):
        return pltpu.roll(v, ex - 1, 0)

    def xm(v):
        return pltpu.roll(v, 1, 0)

    def zp(v):
        return pltpu.roll(v, cz - 1, 1)

    def zm(v):
        return pltpu.roll(v, 1, 1)

    last_z = lax.broadcasted_iota(jnp.int32, (ex, cz), 1) == cz - 1
    own = pl.ds(XH, cx)

    def loop(lo, hi, body):
        def step(y, carry):
            body(y)
            return carry

        lax.fori_loop(lo, hi, step, 0)

    def side_faces(y):
        p = half[y]
        fx = recip(p + xp(p))
        fz = jnp.where(last_z, 0.0, recip(p + zp(p)))
        tx[y] = fx
        tz[y] = fz
        wt[y] = storage + (fx + xm(fx)) + (fz + zm(fz))

    def next_faces(y):
        ty[y] = recip(half[y] + half[y + 1])

    def first(y):
        w = RELAX * recip(wt[y] + ty[y] + ty[y - 1])
        wt[y] = w
        h1[y] = w * src[y]

    def sweep(v_ref, y):
        v = v_ref[y]
        fx, fz = tx[y], tz[y]
        total = src[y] + ty[y] * v_ref[y + 1] + ty[y - 1] * v_ref[y - 1]
        total = total + (fx * xp(v) + xm(fx * v)) + (fz * zp(v) + zm(fz * v))
        return (1.0 - RELAX) * v + wt[y] * total

    def second(y):
        h2[y] = sweep(h1, y)

    landed(half_out[2:4], SIDES[2:4])
    loop(y0, y1, side_faces)
    loop(y0, y1 - 1, next_faces)
    landed(src_out[2:4], SIDES[2:4])
    loop(y0 + 1, y1 - 1, first)
    loop(y0 + 2, y1 - 2, second)
    rest_sides = SIDES[:2] + SIDES[4:]
    landed(half_out[:2] + half_out[4:], rest_sides)
    loop(y0 - 2, y0, side_faces)
    loop(y1, y1 + 2, side_faces)
    loop(y0 - 3, y0, next_faces)
    loop(y1 - 1, y1 + 2, next_faces)
    landed(src_out[:2] + src_out[4:], rest_sides)
    loop(y0 - 2, y0 + 1, first)
    loop(y1 - 1, y1 + 2, first)
    loop(y0 - 1, y0 + 2, second)
    loop(y1 - 2, y1 + 1, second)

    def gather_sum(y, acc):
        inner = src[y, own, :] - storage * h2[y, own, :]
        return acc + jnp.sum(inner.reshape(cx // 8, 8, cz), axis=0)

    acc = lax.fori_loop(y0, y1, gather_sum, jnp.zeros((8, cz), F32))
    edge = ty[y1 - 1, own, :] * (h2[y1 - 1, own, :] - h2[y1, own, :]) + ty[y0 - 1, own, :] * (h2[y0, own, :] - h2[y0 - 1, own, :])
    acc = acc - jnp.sum(edge.reshape(cx // 8, 8, cz), axis=0)
    rows = pl.ds(y0, cy)

    def x_face(x):
        a = tx[rows, pl.ds(x - 7, 8), :][:, 7, :]
        b = h2[rows, pl.ds(x - 7, 8), :][:, 7, :]
        c = h2[rows, pl.ds(x + 1, 8), :][:, 0, :]
        return a * (b - c)

    side = x_face(XH - 1) - x_face(XH + cx - 1)
    acc = acc + jnp.where(lax.broadcasted_iota(jnp.int32, (8, cz), 0) == 0, jnp.sum(side, axis=0, keepdims=True), 0.0)
    rhs = jnp.sum(jnp.sum(acc, axis=0, keepdims=True), axis=1, keepdims=True)
    link_x = jnp.sum(jnp.sum(tx[pl.ds(y0, cy), pl.ds(XH + cx - 8, 8), :][:, 7, :], axis=0, keepdims=True), axis=1, keepdims=True)
    link_y = jnp.sum(jnp.sum(ty[y1 - 1, own, :], axis=0, keepdims=True), axis=1, keepdims=True)
    lane = lax.broadcasted_iota(jnp.int32, (1, 128), 1)
    packed = jnp.where(lane == g, rhs, jnp.where(lane == g + 32, link_x, jnp.where(lane == g + 64, link_y, 0.0)))
    mine[...] = packed
    gath[me] = packed

    def to(other):
        return pltpu.make_async_remote_copy(
            src_ref=mine, dst_ref=gath.at[me], send_sem=cs_sem, recv_sem=cr_sem,
            device_id=(other // tiles, lax.rem(other, tiles)), device_id_type=MESH)

    def tell(k, carry):
        to(lax.rem(me + k, n)).start()
        return carry

    lax.fori_loop(1, n, tell, 0)
    rest = gath.at[pl.ds(0, n - 1)]

    def third(y):
        s2[y, own, :] = sweep(h2, y)[XH:XH + cx]

    four = SIDES[:4]
    s2_out = halo(s2, 1, 2, four)
    loop(y0, y0 + 1, third)
    pl.when(exists(0, -1))(s2_out[1].start)
    loop(y1 - 1, y1, third)
    pl.when(exists(0, 1))(s2_out[0].start)
    loop(y0 + 1, y1 - 1, third)
    begin(s2_out[2:], four[2:])
    pltpu.make_async_copy(rest, rest, cr_sem).wait()

    lanes = lax.broadcasted_iota(jnp.int32, (tiles, 128), 1)
    whole = jnp.sum(gath[...].reshape(groups, tiles, 128), axis=0)
    c_rhs = jnp.where(lanes < groups, whole, 0.0)
    c_lx = jnp.where(lanes < groups, pltpu.roll(whole, 96, 1), 0.0)
    c_ly = jnp.where(lanes < groups, pltpu.roll(whole, 64, 1), 0.0)

    def before(v, s):
        return pltpu.roll(v, s, 0)

    def after(v, s):
        return pltpu.roll(v, tiles - s, 0)

    lx_prev = pltpu.roll(c_lx, 1, 1)
    ly_prev = before(c_ly, 1)
    diag = storage * cx * cy * cz + c_lx + lx_prev + c_ly + ly_prev
    lower, upper = -ly_prev, -c_ly
    steps = []
    stride = 1
    while stride < tiles:
        alpha = -lower / before(diag, stride)
        gamma = -upper / after(diag, stride)
        steps.append((stride, alpha, gamma))
        diag = diag + alpha * before(upper, stride) + gamma * after(lower, stride)
        lower, upper = alpha * before(lower, stride), gamma * after(upper, stride)
        stride *= 2
    inv = 1.0 / diag
    corr = jnp.zeros((tiles, 128), F32)
    for _ in range(COARSE_ITERS):
        r = c_rhs + lx_prev * pltpu.roll(corr, 1, 1) + c_lx * pltpu.roll(corr, 127, 1)
        for stride, alpha, gamma in steps:
            r = r + alpha * before(r, stride) + gamma * after(r, stride)
        corr = r * inv

    row_t = lax.broadcasted_iota(jnp.int32, (tiles, 128), 0)

    def pick(dg, dt):
        hit = jnp.logical_and(row_t == t + dt, lanes == g + dg)
        one = jnp.sum(jnp.where(hit, corr, 0.0), axis=0, keepdims=True)
        return jnp.broadcast_to(jnp.sum(one, axis=1, keepdims=True), (1, cz))

    cols = [[pick(dg, dt) for dg in (-1, 0, 1)] for dt in (-1, 0, 1)]
    xrow = lax.broadcasted_iota(jnp.int32, (ex, cz), 0)

    def spread(line, ahead):
        return jnp.where(xrow < XH - ahead, line[0], jnp.where(xrow < XH + cx - ahead, line[1], line[2]))

    c_low, c_mid, c_high = [spread(line, 0) for line in cols]
    landed(s2_out, four)

    def lift(y, c, line, extra):
        across = tx[y] * (spread(line, 1) - c)
        h4[y] = s2[y] + c + wt[y] * (across - xm(across) - storage * c + extra)

    loop(y0 + 1, y1 - 1, lambda y: lift(y, c_mid, cols[1], 0.0))
    lift(y0 - 1, c_low, cols[0], ty[y0 - 1] * (c_mid - c_low))
    lift(y0, c_mid, cols[1], ty[y0 - 1] * (c_low - c_mid))
    lift(y1 - 1, c_mid, cols[1], ty[y1 - 1] * (c_high - c_mid))
    lift(y1, c_high, cols[2], ty[y1 - 1] * (c_mid - c_high))

    def store(k):
        return pltpu.make_async_copy(res.at[k], out.at[:, k, :], out_sem.at[k])

    for k in range(cy):
        res[k] = sweep(h4, y0 + k)[XH:XH + cx]
        store(k).start()
    left(half_out, SIDES)
    left(src_out, SIDES)
    left(s2_out, four)
    pltpu.make_async_copy(rest, rest, cs_sem).wait()
    for k in range(cy):
        store(k).wait()


def solution(mesh):
    groups, tiles = mesh.shape["group"], mesh.shape["tile"]

    def on_device(facies, table, source):
        cx, cy, cz = source.shape
        ext = pltpu.VMEM((cy + 2 * PW, cx + 2 * XH, cz), F32)
        n = groups * tiles
        return pl.pallas_call(
            functools.partial(kernel, groups, tiles),
            out_shape=jax.ShapeDtypeStruct(source.shape, F32),
            in_specs=[pl.BlockSpec(memory_space=pl.ANY), pl.BlockSpec(memory_space=pltpu.SMEM), pl.BlockSpec(memory_space=pl.ANY)],
            out_specs=pl.BlockSpec(memory_space=pl.ANY),
            scratch_shapes=[
                pltpu.VMEM((cy, cx, cz), jnp.int32),
                ext, ext, ext, ext, ext, ext, ext, ext, ext, ext,
                pltpu.VMEM((cy, cx, cz), F32),
                pltpu.VMEM((1, 128), F32),
                pltpu.VMEM((n, 1, 128), F32),
                pltpu.SemaphoreType.DMA((2 * cy,)),
                pltpu.SemaphoreType.DMA((cy,)),
                pltpu.SemaphoreType.DMA((3, 8)),
                pltpu.SemaphoreType.DMA((3, 8)),
                pltpu.SemaphoreType.DMA,
                pltpu.SemaphoreType.DMA,
            ],
            compiler_params=pltpu.CompilerParams(
                collective_id=0, has_side_effects=True, vmem_limit_bytes=62 * 1024 * 1024),
        )(facies, table, source)

    placed = (P("group", "tile", None), P(), P("group", "tile", None))
    return jax.shard_map(on_device, mesh=mesh, in_specs=placed, out_specs=P("group", "tile", None), check_vma=False)
```

```python
import functools

import jax
import jax.numpy as jnp
from jax import lax
from jax.experimental import pallas as pl
from jax.experimental.pallas import tpu as pltpu
from jax.sharding import PartitionSpec as P

COARSE_ITERS = 3
RELAX = 0.8
MESH = pl.DeviceIdType.MESH
F32 = jnp.float32

XH = 8
FAR = 1e36
SIDES = [(0, 1), (0, -1), (1, 0), (-1, 0)]
SLOT = 16


def recip(x):
    y = pl.reciprocal(x, approx=True)
    return y * (2.0 - x * y)


def kernel(groups, tiles, facies, table, source, out, fac, src, half, tx, ty, tz, wt, h1, h2, s2, h4, res,
           mine, gath, in_sem, out_sem, send_sem, recv_sem, cs_sem, cr_sem):
    cx, cy, cz = source.shape
    nf = table.shape[0]
    n = groups * tiles
    g = lax.axis_index("group")
    t = lax.axis_index("tile")
    me = g * tiles + t
    storage = 0.01 / cy
    own = pl.ds(XH, cx)
    rows = pl.ds(1, cy)

    barrier = pltpu.get_barrier_semaphore()

    def greet(k, carry):
        other = lax.rem(me + k, n)
        pl.semaphore_signal(barrier, inc=1, device_id=(other // tiles, lax.rem(other, tiles)), device_id_type=MESH)
        return carry

    lax.fori_loop(1, n, greet, 0)

    loads_f = [pltpu.make_async_copy(facies.at[:, y, :], fac.at[y], in_sem.at[cy + y]) for y in range(cy)]
    loads_s = [pltpu.make_async_copy(source.at[:, y, :], src.at[y], in_sem.at[y]) for y in range(cy)]
    for c in loads_f + loads_s:
        c.start()

    def exists(dg, dt):
        if dg:
            return g < groups - 1 if dg > 0 else g > 0
        return t < tiles - 1 if dt > 0 else t > 0

    def span(dg, dt):
        ys, yd, yn = {0: (1, 1, cy), 1: (cy, 0, 1), -1: (1, cy + 1, 1)}[dt]
        xs, xd, xn = {0: (XH, XH, cx), 1: (cx, 0, XH), -1: (XH, XH + cx, XH)}[dg]
        return (pl.ds(ys, yn), pl.ds(xs, xn)), (pl.ds(yd, yn), pl.ds(xd, xn))

    def halo(buf, slot):
        copies = []
        for k, (dg, dt) in enumerate(SIDES):
            a, b = span(dg, dt)
            copies.append(pltpu.make_async_remote_copy(
                src_ref=buf.at[a], dst_ref=buf.at[b], send_sem=send_sem.at[slot, k], recv_sem=recv_sem.at[slot, k],
                device_id=(g + dg, t + dt), device_id_type=MESH))
        return copies

    def blank(buf, value):
        for dg, dt in SIDES:
            _, b = span(dg, dt)

            @pl.when(jnp.logical_not(exists(-dg, -dt)))
            def _():
                buf[b] = jnp.full((b[0].size, b[1].size, cz), value, F32)

    def begin(copies, which):
        for k in which:
            pl.when(exists(*SIDES[k]))(copies[k].start)

    def landed(copies, which):
        for k in which:
            dg, dt = SIDES[k]
            pl.when(exists(-dg, -dt))(copies[k].wait_recv)

    def left(copies):
        for c, side in zip(copies, SIDES):
            pl.when(exists(*side))(c.wait_send)

    def loop(lo, hi, body):
        def step(y, carry):
            body(y)
            return carry

        lax.fori_loop(lo, hi, step, 0, unroll=2)

    along_y, along_x = (0, 1), (2, 3)
    blank(half, FAR)
    for buf in (h1, h2, h4):
        blank(buf, 0.0)
    kinds = [0.5 / jnp.full((1, cz), table[k], F32) for k in range(nf)]
    for c in loads_f:
        c.wait()

    def paint(y):
        f = fac[y]
        p = jnp.broadcast_to(kinds[0], (cx, cz))
        for k in range(1, nf):
            p = jnp.where(f == k, kinds[k], p)
        half[y + 1, own, :] = p

    loop(0, cy, paint)
    pl.semaphore_wait(barrier, n - 1)
    half_out, h1_out, h2_out, h4_out = [halo(buf, k) for k, buf in enumerate((half, h1, h2, h4))]
    begin(half_out, along_y)
    begin(half_out, along_x)

    xrow = lax.broadcasted_iota(jnp.int32, (cx, cz), 0)
    zcol = lax.broadcasted_iota(jnp.int32, (cx, cz), 1)

    def xp(v, edge):
        return jnp.where(xrow == cx - 1, edge, pltpu.roll(v, cx - 1, 0))

    def xm(v, edge):
        return jnp.where(xrow == 0, edge, pltpu.roll(v, 1, 0))

    def zp(v):
        return pltpu.roll(v, cz - 1, 1)

    def zm(v):
        return pltpu.roll(v, 1, 1)

    def low(ref, y):
        return ref[y, pl.ds(XH - 1, 1), :]

    def high(ref, y):
        return ref[y, pl.ds(XH + cx, 1), :]

    def z_faces(y):
        p = half[y, own, :]
        fz = jnp.where(zcol == cz - 1, 0.0, recip(p + zp(p)))
        tz[y] = fz
        wt[y] = storage + (fz + zm(fz))

    def y_face(y):
        ty[y] = recip(half[y, own, :] + half[y + 1, own, :])

    def x_faces(y):
        p = half[y, own, :]
        fx = recip(p + xp(p, high(half, y)))
        first_face = recip(low(half, y) + p[0:1])
        tx[y, own, :] = fx
        tx[y, pl.ds(XH - 1, 1), :] = first_face
        wt[y] = wt[y] + (fx + xm(fx, first_face))

    def first(y):
        w = RELAX * recip(wt[y] + ty[y] + ty[y - 1])
        wt[y] = w
        h1[y, own, :] = w * src[y - 1]

    def sweep(v_ref, y):
        v = v_ref[y, own, :]
        fx, fz = tx[y, own, :], tz[y]
        total = src[y - 1] + ty[y] * v_ref[y + 1, own, :] + ty[y - 1] * v_ref[y - 1, own, :]
        total = total + (fx * xp(v, high(v_ref, y)) + xm(fx * v, low(tx, y) * low(v_ref, y)))
        total = total + (fz * zp(v) + zm(fz * v))
        return (1.0 - RELAX) * v + wt[y] * total

    def second(y):
        h2[y, own, :] = sweep(h1, y)

    def third(y):
        s2[y] = sweep(h2, y)

    loop(1, cy + 1, z_faces)
    loop(1, cy, y_face)
    landed(half_out, along_x)
    loop(1, cy + 1, x_faces)
    for c in loads_s:
        c.wait()
    loop(2, cy, first)
    landed(half_out, along_y)
    y_face(0)
    y_face(cy)
    first(1)
    first(cy)
    begin(h1_out, along_y)
    begin(h1_out, along_x)

    def total_of(v):
        return jnp.sum(jnp.sum(v, axis=0, keepdims=True), axis=1, keepdims=True)

    link_x = total_of(tx[rows, pl.ds(XH + cx - 8, 8), :][:, 7, :])
    link_y = total_of(ty[cy])
    landed(h1_out, along_x)
    loop(2, cy, second)
    landed(h1_out, along_y)
    second(1)
    second(cy)
    begin(h2_out, along_y)
    begin(h2_out, along_x)

    def keep(y, acc):
        return acc + (src[y - 1] - storage * h2[y, own, :])

    kept = total_of(lax.fori_loop(1, cy + 1, keep, jnp.zeros((cx, cz), F32), unroll=2))
    y_hi = total_of(ty[cy] * h2[cy, own, :])
    y_lo = total_of(ty[0] * h2[1, own, :])
    x_hi = total_of(tx[rows, pl.ds(XH + cx - 8, 8), :][:, 7, :] * h2[rows, pl.ds(XH + cx - 8, 8), :][:, 7, :])
    x_lo = total_of(tx[rows, pl.ds(0, XH), :][:, XH - 1, :] * h2[rows, pl.ds(XH, 8), :][:, 0, :])
    lane = lax.broadcasted_iota(jnp.int32, (1, 128), 1)
    packed = jnp.zeros((1, 128), F32)
    for k, value in enumerate((kept - y_hi - y_lo - x_hi - x_lo, link_x, link_y, y_hi, y_lo, x_hi, x_lo)):
        packed = jnp.where(lane == g + k * SLOT, value, packed)
    mine[...] = packed
    gath[me] = packed

    def tell(k, carry):
        other = lax.rem(me + k, n)
        pltpu.make_async_remote_copy(
            src_ref=mine, dst_ref=gath.at[me], send_sem=cs_sem, recv_sem=cr_sem,
            device_id=(other // tiles, lax.rem(other, tiles)), device_id_type=MESH).start()
        return carry

    lax.fori_loop(1, n, tell, 0)
    rest = gath.at[pl.ds(0, n - 1)]

    landed(h2_out, along_x)
    loop(2, cy, third)
    landed(h2_out, along_y)
    third(1)
    third(cy)
    pltpu.make_async_copy(rest, rest, cr_sem).wait()

    lanes = lax.broadcasted_iota(jnp.int32, (tiles, 128), 1)
    row_t = lax.broadcasted_iota(jnp.int32, (tiles, 128), 0)
    whole = jnp.sum(gath[...].reshape(groups, tiles, 128), axis=0)

    def before(v, s):
        return pltpu.roll(v, s, 0)

    def after(v, s):
        return pltpu.roll(v, tiles - s, 0)

    def left_of(v):
        return pltpu.roll(v, 1, 1)

    def right_of(v):
        return pltpu.roll(v, 127, 1)

    parts = [jnp.where(lanes < groups, pltpu.roll(whole, (128 - k * SLOT) % 128, 1) if k else whole, 0.0) for k in range(7)]
    c_rhs, c_lx, c_ly, f_yh, f_yl, f_xh, f_xl = parts
    c_rhs = c_rhs + jnp.where(row_t < tiles - 1, after(f_yl, 1), 0.0) + jnp.where(row_t > 0, before(f_yh, 1), 0.0)
    c_rhs = c_rhs + right_of(f_xl) + jnp.where(lanes < groups, left_of(f_xh), 0.0)
    lx_prev = left_of(c_lx)
    ly_prev = before(c_ly, 1)
    diag = storage * cx * cy * cz + c_lx + lx_prev + c_ly + ly_prev
    lower, upper = -ly_prev, -c_ly
    steps = []
    stride = 1
    while stride < tiles:
        alpha = -lower * recip(before(diag, stride))
        gamma = -upper * recip(after(diag, stride))
        steps.append((stride, alpha, gamma))
        diag = diag + alpha * before(upper, stride) + gamma * after(lower, stride)
        lower, upper = alpha * before(lower, stride), gamma * after(upper, stride)
        stride *= 2
    inv = recip(diag)
    corr = None
    for _ in range(COARSE_ITERS):
        r = c_rhs
        if corr is not None:
            r = r + lx_prev * left_of(corr) + c_lx * right_of(corr)
        for stride, alpha, gamma in steps:
            r = r + alpha * before(r, stride) + gamma * after(r, stride)
        corr = r * inv

    def pick(dg, dt):
        hit = jnp.logical_and(row_t == t + dt, lanes == g + dg)
        return jnp.broadcast_to(total_of(jnp.where(hit, corr, 0.0)), (1, cz))

    c_own = pick(0, 0)
    d_low, d_high, d_left, d_right = [pick(dg, dt) - c_own for dg, dt in ((0, -1), (0, 1), (-1, 0), (1, 0))]

    def lift(y, extra):
        more = jnp.where(xrow == cx - 1, tx[y, own, :] * d_right, jnp.where(xrow == 0, low(tx, y) * d_left, 0.0))
        h4[y, own, :] = s2[y] + c_own + wt[y] * (more + extra - storage * c_own)

    lift(1, ty[0] * d_low)
    lift(cy, ty[cy] * d_high)
    begin(h4_out, along_y)
    loop(2, cy, lambda y: lift(y, 0.0))
    begin(h4_out, along_x)

    def store(k):
        return pltpu.make_async_copy(res.at[k], out.at[:, k, :], out_sem.at[k])

    def last(y):
        res[y - 1] = sweep(h4, y)
        store(y - 1).start()

    landed(h4_out, along_x)
    for y in range(2, cy):
        last(y)
    landed(h4_out, along_y)
    last(1)
    last(cy)
    for copies in (half_out, h1_out, h2_out, h4_out):
        left(copies)
    pltpu.make_async_copy(rest, rest, cs_sem).wait()
    for k in range(cy):
        store(k).wait()


def deliver(res, out, sem):
    step = res.shape[0] // sem.shape[0]
    copies = [pltpu.make_async_copy(res.at[pl.ds(k * step, step)], out.at[pl.ds(k * step, step)], sem.at[k])
              for k in range(sem.shape[0])]
    for c in copies:
        c.start()
    for c in copies:
        c.wait()


def solution(mesh):
    groups, tiles = mesh.shape["group"], mesh.shape["tile"]

    def on_device(facies, table, source):
        cx, cy, cz = source.shape
        n = groups * tiles
        grant = pltpu.CompilerParams(vmem_limit_bytes=62 * 1024 * 1024)
        ext = pltpu.VMEM((cy + 2, cx + 2 * XH, cz), F32)
        plain = pltpu.VMEM((cy + 2, cx, cz), F32)
        anywhere = pl.BlockSpec(memory_space=pl.ANY)
        res = pl.pallas_call(
            functools.partial(kernel, groups, tiles),
            out_shape=jax.ShapeDtypeStruct(source.shape, F32),
            in_specs=[anywhere, pl.BlockSpec(memory_space=pltpu.SMEM), anywhere],
            out_specs=anywhere,
            scratch_shapes=[
                pltpu.VMEM((cy, cx, cz), jnp.int32),
                pltpu.VMEM((cy, cx, cz), F32),
                ext, ext, plain, plain, plain, ext, ext, plain, ext,
                pltpu.VMEM((cy, cx, cz), F32),
                pltpu.VMEM((1, 128), F32),
                pltpu.VMEM((n, 1, 128), F32),
                pltpu.SemaphoreType.DMA((2 * cy,)),
                pltpu.SemaphoreType.DMA((cy,)),
                pltpu.SemaphoreType.DMA((4, 4)),
                pltpu.SemaphoreType.DMA((4, 4)),
                pltpu.SemaphoreType.DMA,
                pltpu.SemaphoreType.DMA,
            ],
            compiler_params=pltpu.CompilerParams(
                collective_id=0, has_side_effects=True, vmem_limit_bytes=62 * 1024 * 1024),
        )(facies, table, source)
        return pl.pallas_call(
            deliver,
            out_shape=jax.ShapeDtypeStruct(source.shape, F32),
            in_specs=[anywhere],
            out_specs=anywhere,
            scratch_shapes=[pltpu.SemaphoreType.DMA((8,))],
            compiler_params=grant,
        )(res)

    placed = (P("group", "tile", None), P(), P("group", "tile", None))
    return jax.shard_map(on_device, mesh=mesh, in_specs=placed, out_specs=P("group", "tile", None), check_vma=False)
```

```python
import functools

import jax
import jax.numpy as jnp
from jax import lax
from jax.experimental import pallas as pl
from jax.experimental.pallas import tpu as pltpu
from jax.sharding import PartitionSpec as P

COARSE_ITERS = 3
RELAX = 0.8
MESH = pl.DeviceIdType.MESH
F32 = jnp.float32

XH = 8
FAR = 1e36
SIDES = [(0, 1), (0, -1), (1, 0), (-1, 0)]
SLOT = 16
NEAR = 4


def recip(x):
    y = pl.reciprocal(x, approx=True)
    return y * (2.0 - x * y)


def kernel(groups, tiles, facies, table, source, out, fac, src, half, tx, ty, tz, wt, h1, h2, s2, h4, res,
           mine, gath, in_sem, out_sem, send_sem, recv_sem, cs_sem, cr_sem):
    cx, cy, cz = source.shape
    nf = table.shape[0]
    g = lax.axis_index("group")
    t = lax.axis_index("tile")
    storage = 0.01 / cy
    own = pl.ds(XH, cx)
    rows = pl.ds(1, cy)

    barrier = pltpu.get_barrier_semaphore()

    quads, j, q = tiles // NEAR, lax.rem(t, NEAR), t // NEAR
    team = groups * NEAR
    seat = g * NEAR + j

    def mate(k):
        other = lax.rem(seat + k, team)
        return (other // NEAR, q * NEAR + lax.rem(other, NEAR))

    def peer(k):
        return (g, lax.rem(q + k, quads) * NEAR + j)

    def for_each(count, act):
        def step(k, carry):
            act(k)
            return carry

        lax.fori_loop(1, count, step, 0)

    def greet(device):
        pl.semaphore_signal(barrier, inc=1, device_id=device, device_id_type=MESH)

    for_each(team, lambda k: greet(mate(k)))
    for_each(quads, lambda k: greet(peer(k)))
    next_far = jnp.logical_and(j == NEAR - 1, t < tiles - 1)
    prev_far = jnp.logical_and(j == 0, t > 0)
    pl.when(next_far)(lambda: greet((g, t + 1)))
    pl.when(prev_far)(lambda: greet((g, t - 1)))

    loads_f = [pltpu.make_async_copy(facies.at[:, y, :], fac.at[y], in_sem.at[cy + y]) for y in range(cy)]
    loads_s = [pltpu.make_async_copy(source.at[:, y, :], src.at[y], in_sem.at[y]) for y in range(cy)]
    for c in loads_f + loads_s:
        c.start()

    def exists(dg, dt):
        if dg:
            return g < groups - 1 if dg > 0 else g > 0
        return t < tiles - 1 if dt > 0 else t > 0

    def span(dg, dt):
        ys, yd, yn = {0: (1, 1, cy), 1: (cy, 0, 1), -1: (1, cy + 1, 1)}[dt]
        xs, xd, xn = {0: (XH, XH, cx), 1: (cx, 0, XH), -1: (XH, XH + cx, XH)}[dg]
        return (pl.ds(ys, yn), pl.ds(xs, xn)), (pl.ds(yd, yn), pl.ds(xd, xn))

    def halo(buf, slot):
        copies = []
        for k, (dg, dt) in enumerate(SIDES):
            a, b = span(dg, dt)
            copies.append(pltpu.make_async_remote_copy(
                src_ref=buf.at[a], dst_ref=buf.at[b], send_sem=send_sem.at[slot, k], recv_sem=recv_sem.at[slot, k],
                device_id=(g + dg, t + dt), device_id_type=MESH))
        return copies

    def blank(buf, value):
        for dg, dt in SIDES:
            _, b = span(dg, dt)

            @pl.when(jnp.logical_not(exists(-dg, -dt)))
            def _():
                buf[b] = jnp.full((b[0].size, b[1].size, cz), value, F32)

    def begin(copies, which):
        for k in which:
            pl.when(exists(*SIDES[k]))(copies[k].start)

    def landed(copies, which):
        for k in which:
            dg, dt = SIDES[k]
            pl.when(exists(-dg, -dt))(copies[k].wait_recv)

    def left(copies):
        for c, side in zip(copies, SIDES):
            pl.when(exists(*side))(c.wait_send)

    def loop(lo, hi, body):
        def step(y, carry):
            body(y)
            return carry

        lax.fori_loop(lo, hi, step, 0, unroll=2)

    along_y, along_x = (0, 1), (2, 3)
    blank(half, FAR)
    for buf in (h1, h2, h4):
        blank(buf, 0.0)
    kinds = [0.5 / jnp.full((1, cz), table[k], F32) for k in range(nf)]
    for c in loads_f:
        c.wait()

    def paint(y):
        f = fac[y]
        p = jnp.broadcast_to(kinds[0], (cx, cz))
        for k in range(1, nf):
            p = jnp.where(f == k, kinds[k], p)
        half[y + 1, own, :] = p

    loop(0, cy, paint)
    pl.semaphore_wait(barrier, team + quads - 2 + next_far.astype(jnp.int32) + prev_far.astype(jnp.int32))
    half_out, h1_out, h2_out, h4_out = [halo(buf, k) for k, buf in enumerate((half, h1, h2, h4))]
    begin(half_out, along_y)
    begin(half_out, along_x)

    xrow = lax.broadcasted_iota(jnp.int32, (cx, cz), 0)
    zcol = lax.broadcasted_iota(jnp.int32, (cx, cz), 1)

    def xp(v, edge):
        return jnp.where(xrow == cx - 1, edge, pltpu.roll(v, cx - 1, 0))

    def xm(v, edge):
        return jnp.where(xrow == 0, edge, pltpu.roll(v, 1, 0))

    def zp(v):
        return pltpu.roll(v, cz - 1, 1)

    def zm(v):
        return pltpu.roll(v, 1, 1)

    def low(ref, y):
        return ref[y, pl.ds(XH - 1, 1), :]

    def high(ref, y):
        return ref[y, pl.ds(XH + cx, 1), :]

    def z_faces(y):
        p = half[y, own, :]
        fz = jnp.where(zcol == cz - 1, 0.0, recip(p + zp(p)))
        tz[y] = fz
        wt[y] = storage + (fz + zm(fz))

    def y_face(y):
        ty[y] = recip(half[y, own, :] + half[y + 1, own, :])

    def x_faces(y):
        p = half[y, own, :]
        fx = recip(p + xp(p, high(half, y)))
        first_face = recip(low(half, y) + p[0:1])
        tx[y, own, :] = fx
        tx[y, pl.ds(XH - 1, 1), :] = first_face
        wt[y] = wt[y] + (fx + xm(fx, first_face))

    def first(y):
        w = RELAX * recip(wt[y] + ty[y] + ty[y - 1])
        wt[y] = w
        h1[y, own, :] = w * src[y - 1]

    def sweep(v_ref, y):
        v = v_ref[y, own, :]
        fx, fz = tx[y, own, :], tz[y]
        total = src[y - 1] + ty[y] * v_ref[y + 1, own, :] + ty[y - 1] * v_ref[y - 1, own, :]
        total = total + (fx * xp(v, high(v_ref, y)) + xm(fx * v, low(tx, y) * low(v_ref, y)))
        total = total + (fz * zp(v) + zm(fz * v))
        return (1.0 - RELAX) * v + wt[y] * total

    def second(y):
        h2[y, own, :] = sweep(h1, y)

    def third(y):
        s2[y] = sweep(h2, y)

    loop(1, cy + 1, z_faces)
    loop(1, cy, y_face)
    landed(half_out, along_x)
    loop(1, cy + 1, x_faces)
    for c in loads_s:
        c.wait()
    loop(2, cy, first)
    landed(half_out, along_y)
    y_face(0)
    y_face(cy)
    first(1)
    first(cy)
    begin(h1_out, along_y)
    begin(h1_out, along_x)

    def total_of(v):
        return jnp.sum(jnp.sum(v, axis=0, keepdims=True), axis=1, keepdims=True)

    link_x = total_of(tx[rows, pl.ds(XH + cx - 8, 8), :][:, 7, :])
    link_y = total_of(ty[cy])
    landed(h1_out, along_x)
    loop(2, cy, second)
    landed(h1_out, along_y)
    second(1)
    second(cy)
    begin(h2_out, along_y)
    begin(h2_out, along_x)

    def keep(y, acc):
        return acc + (src[y - 1] - storage * h2[y, own, :])

    kept = total_of(lax.fori_loop(1, cy + 1, keep, jnp.zeros((cx, cz), F32), unroll=2))
    y_hi = total_of(ty[cy] * h2[cy, own, :])
    y_lo = total_of(ty[0] * h2[1, own, :])
    x_hi = total_of(tx[rows, pl.ds(XH + cx - 8, 8), :][:, 7, :] * h2[rows, pl.ds(XH + cx - 8, 8), :][:, 7, :])
    x_lo = total_of(tx[rows, pl.ds(0, XH), :][:, XH - 1, :] * h2[rows, pl.ds(XH, 8), :][:, 0, :])
    lane = lax.broadcasted_iota(jnp.int32, (1, 128), 1)
    packed = jnp.zeros((1, 128), F32)
    for k, value in enumerate((kept - y_hi - y_lo - x_hi - x_lo, link_x, link_y, y_hi, y_lo, x_hi, x_lo)):
        packed = jnp.where(lane == g + k * SLOT, value, packed)
    mine[...] = packed
    gath[q, seat] = packed


    def to_mate(k):
        pltpu.make_async_remote_copy(
            src_ref=mine, dst_ref=gath.at[q, seat], send_sem=cs_sem.at[0], recv_sem=cr_sem.at[0],
            device_id=mate(k), device_id_type=MESH).start()

    def to_peer(k):
        pltpu.make_async_remote_copy(
            src_ref=gath.at[q], dst_ref=gath.at[q], send_sem=cs_sem.at[1], recv_sem=cr_sem.at[1],
            device_id=peer(k), device_id_type=MESH).start()

    for_each(team, to_mate)
    near = gath.at[0, pl.ds(0, team - 1)]
    far = gath.at[pl.ds(0, quads - 1)]

    pltpu.make_async_copy(near, near, cr_sem.at[0]).wait()
    for_each(quads, to_peer)
    landed(h2_out, along_x)
    loop(2, cy, third)
    landed(h2_out, along_y)
    third(1)
    third(cy)
    pltpu.make_async_copy(far, far, cr_sem.at[1]).wait()

    lanes = lax.broadcasted_iota(jnp.int32, (tiles, 128), 1)
    row_t = lax.broadcasted_iota(jnp.int32, (tiles, 128), 0)
    whole = jnp.sum(gath[...].reshape(quads, groups, NEAR, 128), axis=1).reshape(tiles, 128)

    def before(v, s):
        return pltpu.roll(v, s, 0)

    def after(v, s):
        return pltpu.roll(v, tiles - s, 0)

    def left_of(v):
        return pltpu.roll(v, 1, 1)

    def right_of(v):
        return pltpu.roll(v, 127, 1)

    parts = [jnp.where(lanes < groups, pltpu.roll(whole, (128 - k * SLOT) % 128, 1) if k else whole, 0.0) for k in range(7)]
    c_rhs, c_lx, c_ly, f_yh, f_yl, f_xh, f_xl = parts
    c_rhs = c_rhs + jnp.where(row_t < tiles - 1, after(f_yl, 1), 0.0) + jnp.where(row_t > 0, before(f_yh, 1), 0.0)
    c_rhs = c_rhs + right_of(f_xl) + jnp.where(lanes < groups, left_of(f_xh), 0.0)
    lx_prev = left_of(c_lx)
    ly_prev = before(c_ly, 1)
    diag = storage * cx * cy * cz + c_lx + lx_prev + c_ly + ly_prev
    lower, upper = -ly_prev, -c_ly
    steps = []
    stride = 1
    while stride < tiles:
        alpha = -lower * recip(before(diag, stride))
        gamma = -upper * recip(after(diag, stride))
        steps.append((stride, alpha, gamma))
        diag = diag + alpha * before(upper, stride) + gamma * after(lower, stride)
        lower, upper = alpha * before(lower, stride), gamma * after(upper, stride)
        stride *= 2
    inv = recip(diag)
    corr = None
    for _ in range(COARSE_ITERS):
        r = c_rhs
        if corr is not None:
            r = r + lx_prev * left_of(corr) + c_lx * right_of(corr)
        for stride, alpha, gamma in steps:
            r = r + alpha * before(r, stride) + gamma * after(r, stride)
        corr = r * inv

    def pick(dg, dt):
        hit = jnp.logical_and(row_t == t + dt, lanes == g + dg)
        return jnp.broadcast_to(total_of(jnp.where(hit, corr, 0.0)), (1, cz))

    c_own = pick(0, 0)
    d_low, d_high, d_left, d_right = [pick(dg, dt) - c_own for dg, dt in ((0, -1), (0, 1), (-1, 0), (1, 0))]

    def lift(y, extra):
        more = jnp.where(xrow == cx - 1, tx[y, own, :] * d_right, jnp.where(xrow == 0, low(tx, y) * d_left, 0.0))
        h4[y, own, :] = s2[y] + c_own + wt[y] * (more + extra - storage * c_own)

    lift(1, ty[0] * d_low)
    lift(cy, ty[cy] * d_high)
    begin(h4_out, along_y)
    loop(2, cy, lambda y: lift(y, 0.0))
    begin(h4_out, along_x)

    def store(k):
        return pltpu.make_async_copy(res.at[k], out.at[:, k, :], out_sem.at[k])

    def last(y):
        res[y - 1] = sweep(h4, y)
        store(y - 1).start()

    landed(h4_out, along_x)
    for y in range(2, cy):
        last(y)
    landed(h4_out, along_y)
    last(1)
    last(cy)
    for copies in (half_out, h1_out, h2_out, h4_out):
        left(copies)
    pltpu.make_async_copy(near, near, cs_sem.at[0]).wait()
    pltpu.make_async_copy(far, far, cs_sem.at[1]).wait()
    for k in range(cy):
        store(k).wait()


def solution(mesh):
    groups, tiles = mesh.shape["group"], mesh.shape["tile"]

    def on_device(facies, table, source):
        cx, cy, cz = source.shape
        ext = pltpu.VMEM((cy + 2, cx + 2 * XH, cz), F32)
        plain = pltpu.VMEM((cy + 2, cx, cz), F32)
        anywhere = pl.BlockSpec(memory_space=pl.ANY)
        return pl.pallas_call(
            functools.partial(kernel, groups, tiles),
            out_shape=jax.ShapeDtypeStruct(source.shape, F32),
            in_specs=[anywhere, pl.BlockSpec(memory_space=pltpu.SMEM), anywhere],
            out_specs=anywhere,
            scratch_shapes=[
                pltpu.VMEM((cy, cx, cz), jnp.int32),
                pltpu.VMEM((cy, cx, cz), F32),
                ext, ext, plain, plain, plain, ext, ext, plain, ext,
                pltpu.VMEM((cy, cx, cz), F32),
                pltpu.VMEM((1, 128), F32),
                pltpu.VMEM((tiles // NEAR, groups * NEAR, 1, 128), F32),
                pltpu.SemaphoreType.DMA((2 * cy,)),
                pltpu.SemaphoreType.DMA((cy,)),
                pltpu.SemaphoreType.DMA((4, 4)),
                pltpu.SemaphoreType.DMA((4, 4)),
                pltpu.SemaphoreType.DMA((2,)),
                pltpu.SemaphoreType.DMA((2,)),
            ],
            compiler_params=pltpu.CompilerParams(
                collective_id=0, has_side_effects=True, vmem_limit_bytes=62 * 1024 * 1024),
        )(facies, table, source)

    placed = (P("group", "tile", None), P(), P("group", "tile", None))
    return jax.shard_map(on_device, mesh=mesh, in_specs=placed, out_specs=P("group", "tile", None), check_vma=False)
```

```python
import functools

import jax
import jax.numpy as jnp
from jax import lax
from jax.experimental import pallas as pl
from jax.experimental.pallas import tpu as pltpu
from jax.sharding import PartitionSpec as P

COARSE_ITERS = 3
RELAX = 0.8
MESH = pl.DeviceIdType.MESH
F32 = jnp.float32

PW = 3
SW = 2
XH = 8
SIDES = [(0, 1), (0, -1), (1, 0), (-1, 0), (1, 1), (1, -1), (-1, 1), (-1, -1)]


FAR = 1e36


def recip(x):
    y = pl.reciprocal(x, approx=True)
    return y * (2.0 - x * y)


def kernel(groups, tiles, facies, table, source, out, raw_f, raw_s, half, src, tx, ty, tz, wt, h1, h2, h4, s2, res,
           mine, gath, in_sem, out_sem, send_sem, recv_sem, cs_sem, cr_sem):
    cx, cy, cz = source.shape
    nf = table.shape[0]
    n = groups * tiles
    g = lax.axis_index("group")
    t = lax.axis_index("tile")
    me = g * tiles + t
    ex = cx + 2 * XH
    y0, y1 = PW, PW + cy
    storage = 0.01 / cy

    barrier = pltpu.get_barrier_semaphore()

    def greet(k, carry):
        other = lax.rem(me + k, n)
        pl.semaphore_signal(barrier, inc=1, device_id=(other // tiles, lax.rem(other, tiles)), device_id_type=MESH)
        return carry

    lax.fori_loop(1, n, greet, 0)

    piece = cx // 4
    loads_f = [pltpu.make_async_copy(facies.at[pl.ds(k * piece, piece)], raw_f.at[pl.ds(k * piece, piece)], in_sem.at[k]) for k in range(4)]
    loads_s = [pltpu.make_async_copy(source.at[pl.ds(k * piece, piece)], raw_s.at[pl.ds(k * piece, piece)], in_sem.at[4 + k]) for k in range(4)]
    for c in loads_f + loads_s:
        c.start()

    def exists(dg, dt):
        ok = None
        for pos, d, count in ((g, dg, groups), (t, dt, tiles)):
            if d:
                one = pos < count - 1 if d > 0 else pos > 0
                ok = one if ok is None else jnp.logical_and(ok, one)
        return ok

    def span(dg, dt, w):
        ys, yd, yn = {0: (y0, y0, cy), 1: (y1 - w, y0 - w, w), -1: (y0, y1, w)}[dt]
        xs, xd, xn = {0: (XH, XH, cx), 1: (cx, 0, XH), -1: (XH, XH + cx, XH)}[dg]
        return (pl.ds(ys, yn), pl.ds(xs, xn)), (pl.ds(yd, yn), pl.ds(xd, xn))

    def halo(buf, w, slot, sides):
        copies = []
        for k, (dg, dt) in enumerate(sides):
            a, b = span(dg, dt, w)
            copies.append(pltpu.make_async_remote_copy(
                src_ref=buf.at[a], dst_ref=buf.at[b], send_sem=send_sem.at[slot, k], recv_sem=recv_sem.at[slot, k],
                device_id=(g + dg, t + dt), device_id_type=MESH))
        return copies

    def blank(buf, w, sides, value):
        for dg, dt in sides:
            _, b = span(dg, dt, w)

            @pl.when(jnp.logical_not(exists(-dg, -dt)))
            def _():
                buf[b] = jnp.full((b[0].size, b[1].size, cz), value, F32)

    def begin(copies, sides):
        for c, (dg, dt) in zip(copies, sides):
            pl.when(exists(dg, dt))(c.start)

    def landed(copies, sides):
        for c, (dg, dt) in zip(copies, sides):
            pl.when(exists(-dg, -dt))(c.wait_recv)

    def left(copies, sides):
        for c, (dg, dt) in zip(copies, sides):
            pl.when(exists(dg, dt))(c.wait_send)

    blank(half, PW, SIDES, FAR)
    blank(src, SW, SIDES, 0.0)
    blank(s2, 1, SIDES[:4], 0.0)
    kinds = [0.5 / jnp.full((1, cz), table[k], F32) for k in range(nf)]
    for c in loads_f:
        c.wait()

    def paint(y):
        f = raw_f[:, y, :]
        p = jnp.broadcast_to(kinds[0], (cx, cz))
        for k in range(1, nf):
            p = jnp.where(f == k, kinds[k], p)
        half[y0 + y, pl.ds(XH, cx), :] = p

    for y in range(cy):
        paint(y)
    pl.semaphore_wait(barrier, n - 1)
    half_out = halo(half, PW, 0, SIDES)
    src_out = halo(src, SW, 1, SIDES)
    begin(half_out, SIDES)
    for c in loads_s:
        c.wait()
    for y in range(cy):
        src[y0 + y, pl.ds(XH, cx), :] = raw_s[:, y, :]
    begin(src_out, SIDES)

    def xp(v):
        return pltpu.roll(v, ex - 1, 0)

    def xm(v):
        return pltpu.roll(v, 1, 0)

    def zp(v):
        return pltpu.roll(v, cz - 1, 1)

    def zm(v):
        return pltpu.roll(v, 1, 1)

    last_z = lax.broadcasted_iota(jnp.int32, (ex, cz), 1) == cz - 1
    own = pl.ds(XH, cx)

    def loop(lo, hi, body):
        def step(y, carry):
            body(y)
            return carry

        lax.fori_loop(lo, hi, step, 0, unroll=2)

    def side_faces(y):
        p = half[y]
        fx = recip(p + xp(p))
        fz = jnp.where(last_z, 0.0, recip(p + zp(p)))
        tx[y] = fx
        tz[y] = fz
        wt[y] = storage + (fx + xm(fx)) + (fz + zm(fz))

    def next_faces(y):
        ty[y] = recip(half[y] + half[y + 1])

    def first(y):
        w = RELAX * recip(wt[y] + ty[y] + ty[y - 1])
        wt[y] = w
        h1[y] = w * src[y]

    def sweep(v_ref, y):
        v = v_ref[y]
        fx, fz = tx[y], tz[y]
        total = src[y] + ty[y] * v_ref[y + 1] + ty[y - 1] * v_ref[y - 1]
        total = total + (fx * xp(v) + xm(fx * v)) + (fz * zp(v) + zm(fz * v))
        return (1.0 - RELAX) * v + wt[y] * total

    def second(y):
        h2[y] = sweep(h1, y)

    landed(half_out[2:4], SIDES[2:4])
    loop(y0, y1, side_faces)
    loop(y0, y1 - 1, next_faces)
    landed(src_out[2:4], SIDES[2:4])
    loop(y0 + 1, y1 - 1, first)
    loop(y0 + 2, y1 - 2, second)
    rest_sides = SIDES[:2] + SIDES[4:]
    landed(half_out[:2] + half_out[4:], rest_sides)
    loop(y0 - 2, y0, side_faces)
    loop(y1, y1 + 2, side_faces)
    loop(y0 - 3, y0, next_faces)
    loop(y1 - 1, y1 + 2, next_faces)
    landed(src_out[:2] + src_out[4:], rest_sides)
    loop(y0 - 2, y0 + 1, first)
    loop(y1 - 1, y1 + 2, first)
    loop(y0 - 1, y0 + 2, second)
    loop(y1 - 2, y1 + 1, second)

    def gather_sum(y, acc):
        inner = src[y, own, :] - storage * h2[y, own, :]
        return acc + jnp.sum(inner.reshape(cx // 8, 8, cz), axis=0)

    acc = lax.fori_loop(y0, y1, gather_sum, jnp.zeros((8, cz), F32), unroll=4)
    edge = ty[y1 - 1, own, :] * (h2[y1 - 1, own, :] - h2[y1, own, :]) + ty[y0 - 1, own, :] * (h2[y0, own, :] - h2[y0 - 1, own, :])
    acc = acc - jnp.sum(edge.reshape(cx // 8, 8, cz), axis=0)
    rows = pl.ds(y0, cy)

    def x_face(x):
        a = tx[rows, pl.ds(x - 7, 8), :][:, 7, :]
        b = h2[rows, pl.ds(x - 7, 8), :][:, 7, :]
        c = h2[rows, pl.ds(x + 1, 8), :][:, 0, :]
        return a * (b - c)

    side = x_face(XH - 1) - x_face(XH + cx - 1)
    acc = acc + jnp.where(lax.broadcasted_iota(jnp.int32, (8, cz), 0) == 0, jnp.sum(side, axis=0, keepdims=True), 0.0)
    rhs = jnp.sum(jnp.sum(acc, axis=0, keepdims=True), axis=1, keepdims=True)
    link_x = jnp.sum(jnp.sum(tx[pl.ds(y0, cy), pl.ds(XH + cx - 8, 8), :][:, 7, :], axis=0, keepdims=True), axis=1, keepdims=True)
    link_y = jnp.sum(jnp.sum(ty[y1 - 1, own, :], axis=0, keepdims=True), axis=1, keepdims=True)
    lane = lax.broadcasted_iota(jnp.int32, (1, 128), 1)
    packed = jnp.where(lane == g, rhs, jnp.where(lane == g + 32, link_x, jnp.where(lane == g + 64, link_y, 0.0)))
    mine[...] = packed
    gath[me] = packed

    def to(other):
        return pltpu.make_async_remote_copy(
            src_ref=mine, dst_ref=gath.at[me], send_sem=cs_sem, recv_sem=cr_sem,
            device_id=(other // tiles, lax.rem(other, tiles)), device_id_type=MESH)

    def tell(k, carry):
        to(lax.rem(me + k, n)).start()
        return carry

    lax.fori_loop(1, n, tell, 0)
    rest = gath.at[pl.ds(0, n - 1)]

    def third(y):
        s2[y, own, :] = sweep(h2, y)[XH:XH + cx]

    four = SIDES[:4]
    s2_out = halo(s2, 1, 2, four)
    loop(y0, y0 + 1, third)
    pl.when(exists(0, -1))(s2_out[1].start)
    loop(y1 - 1, y1, third)
    pl.when(exists(0, 1))(s2_out[0].start)
    loop(y0 + 1, y1 - 1, third)
    begin(s2_out[2:], four[2:])
    pltpu.make_async_copy(rest, rest, cr_sem).wait()

    lanes = lax.broadcasted_iota(jnp.int32, (tiles, 128), 1)
    whole = jnp.sum(gath[...].reshape(groups, tiles, 128), axis=0)
    c_rhs = jnp.where(lanes < groups, whole, 0.0)
    c_lx = jnp.where(lanes < groups, pltpu.roll(whole, 96, 1), 0.0)
    c_ly = jnp.where(lanes < groups, pltpu.roll(whole, 64, 1), 0.0)

    def before(v, s):
        return pltpu.roll(v, s, 0)

    def after(v, s):
        return pltpu.roll(v, tiles - s, 0)

    lx_prev = pltpu.roll(c_lx, 1, 1)
    ly_prev = before(c_ly, 1)
    diag = storage * cx * cy * cz + c_lx + lx_prev + c_ly + ly_prev
    lower, upper = -ly_prev, -c_ly
    steps = []
    stride = 1
    while stride < tiles:
        alpha = -lower / before(diag, stride)
        gamma = -upper / after(diag, stride)
        steps.append((stride, alpha, gamma))
        diag = diag + alpha * before(upper, stride) + gamma * after(lower, stride)
        lower, upper = alpha * before(lower, stride), gamma * after(upper, stride)
        stride *= 2
    inv = 1.0 / diag
    corr = jnp.zeros((tiles, 128), F32)
    for _ in range(COARSE_ITERS):
        r = c_rhs + lx_prev * pltpu.roll(corr, 1, 1) + c_lx * pltpu.roll(corr, 127, 1)
        for stride, alpha, gamma in steps:
            r = r + alpha * before(r, stride) + gamma * after(r, stride)
        corr = r * inv

    row_t = lax.broadcasted_iota(jnp.int32, (tiles, 128), 0)

    def pick(dg, dt):
        hit = jnp.logical_and(row_t == t + dt, lanes == g + dg)
        one = jnp.sum(jnp.where(hit, corr, 0.0), axis=0, keepdims=True)
        return jnp.broadcast_to(jnp.sum(one, axis=1, keepdims=True), (1, cz))

    cols = [[pick(dg, dt) for dg in (-1, 0, 1)] for dt in (-1, 0, 1)]
    xrow = lax.broadcasted_iota(jnp.int32, (ex, cz), 0)

    def spread(line, ahead):
        return jnp.where(xrow < XH - ahead, line[0], jnp.where(xrow < XH + cx - ahead, line[1], line[2]))

    c_low, c_mid, c_high = [spread(line, 0) for line in cols]
    landed(s2_out, four)

    def lift(y, c, line, extra):
        across = tx[y] * (spread(line, 1) - c)
        h4[y] = s2[y] + c + wt[y] * (across - xm(across) - storage * c + extra)

    loop(y0 + 1, y1 - 1, lambda y: lift(y, c_mid, cols[1], 0.0))
    lift(y0 - 1, c_low, cols[0], ty[y0 - 1] * (c_mid - c_low))
    lift(y0, c_mid, cols[1], ty[y0 - 1] * (c_low - c_mid))
    lift(y1 - 1, c_mid, cols[1], ty[y1 - 1] * (c_high - c_mid))
    lift(y1, c_high, cols[2], ty[y1 - 1] * (c_mid - c_high))

    def store(k):
        return pltpu.make_async_copy(res.at[k], out.at[k], out_sem.at[k])

    for k in range(cy):
        res[k] = sweep(h4, y0 + k)[XH:XH + cx]
        store(k).start()
    left(half_out, SIDES)
    left(src_out, SIDES)
    left(s2_out, four)
    pltpu.make_async_copy(rest, rest, cs_sem).wait()
    for k in range(cy):
        store(k).wait()


def turn(rows, out):
    for y in range(rows.shape[0]):
        out[:, y, :] = rows[y]


def solution(mesh):
    groups, tiles = mesh.shape["group"], mesh.shape["tile"]

    def on_device(facies, table, source):
        cx, cy, cz = source.shape
        ext = pltpu.VMEM((cy + 2 * PW, cx + 2 * XH, cz), F32)
        n = groups * tiles
        res = pl.pallas_call(
            functools.partial(kernel, groups, tiles),
            out_shape=jax.ShapeDtypeStruct((cy, cx, cz), F32),
            in_specs=[pl.BlockSpec(memory_space=pl.ANY), pl.BlockSpec(memory_space=pltpu.SMEM), pl.BlockSpec(memory_space=pl.ANY)],
            out_specs=pl.BlockSpec(memory_space=pl.ANY),
            scratch_shapes=[
                pltpu.VMEM((cx, cy, cz), jnp.int32),
                pltpu.VMEM((cx, cy, cz), F32),
                ext, ext, ext, ext, ext, ext, ext, ext, ext, ext,
                pltpu.VMEM((cy, cx, cz), F32),
                pltpu.VMEM((1, 128), F32),
                pltpu.VMEM((n, 1, 128), F32),
                pltpu.SemaphoreType.DMA((8,)),
                pltpu.SemaphoreType.DMA((cy,)),
                pltpu.SemaphoreType.DMA((3, 8)),
                pltpu.SemaphoreType.DMA((3, 8)),
                pltpu.SemaphoreType.DMA,
                pltpu.SemaphoreType.DMA,
            ],
            compiler_params=pltpu.CompilerParams(
                collective_id=0, has_side_effects=True, vmem_limit_bytes=62 * 1024 * 1024),
        )(facies, table, source)
        part = cx // 4
        return pl.pallas_call(
            turn,
            grid=(4,),
            out_shape=jax.ShapeDtypeStruct(source.shape, F32),
            in_specs=[pl.BlockSpec((cy, part, cz), lambda k: (0, k, 0))],
            out_specs=pl.BlockSpec((part, cy, cz), lambda k: (k, 0, 0)),
            compiler_params=pltpu.CompilerParams(vmem_limit_bytes=62 * 1024 * 1024),
        )(res)

    placed = (P("group", "tile", None), P(), P("group", "tile", None))
    return jax.shard_map(on_device, mesh=mesh, in_specs=placed, out_specs=P("group", "tile", None), check_vma=False)
```

```python
import functools

import jax
import jax.numpy as jnp
from jax import lax
from jax.experimental import pallas as pl
from jax.experimental.pallas import tpu as pltpu
from jax.sharding import PartitionSpec as P

COARSE_ITERS = 3
RELAX = 0.8
MESH = pl.DeviceIdType.MESH
F32 = jnp.float32

PW = 3
SW = 2
XH = 8
SIDES = [(0, 1), (0, -1), (1, 0), (-1, 0), (1, 1), (1, -1), (-1, 1), (-1, -1)]


FAR = 1e36


def recip(x):
    y = pl.reciprocal(x, approx=True)
    return y * (2.0 - x * y)


def kernel(groups, tiles, facies, table, source, out, raw_f, raw_s, half, src, tx, ty, tz, wt, h1, h2, h4, s2, res,
           mine, gath, in_sem, out_sem, send_sem, recv_sem, cs_sem, cr_sem):
    cx, cy, cz = source.shape
    nf = table.shape[0]
    n = groups * tiles
    g = lax.axis_index("group")
    t = lax.axis_index("tile")
    me = g * tiles + t
    ex = cx + 2 * XH
    y0, y1 = PW, PW + cy
    storage = 0.01 / cy

    barrier = pltpu.get_barrier_semaphore()

    def greet(k, carry):
        other = lax.rem(me + k, n)
        pl.semaphore_signal(barrier, inc=1, device_id=(other // tiles, lax.rem(other, tiles)), device_id_type=MESH)
        return carry

    lax.fori_loop(1, n, greet, 0)

    piece = cx // 4
    loads_f = [pltpu.make_async_copy(facies.at[pl.ds(k * piece, piece)], raw_f.at[pl.ds(k * piece, piece)], in_sem.at[k]) for k in range(4)]
    loads_s = [pltpu.make_async_copy(source.at[pl.ds(k * piece, piece)], raw_s.at[pl.ds(k * piece, piece)], in_sem.at[4 + k]) for k in range(4)]
    for c in loads_f + loads_s:
        c.start()

    def exists(dg, dt):
        ok = None
        for pos, d, count in ((g, dg, groups), (t, dt, tiles)):
            if d:
                one = pos < count - 1 if d > 0 else pos > 0
                ok = one if ok is None else jnp.logical_and(ok, one)
        return ok

    def span(dg, dt, w):
        ys, yd, yn = {0: (y0, y0, cy), 1: (y1 - w, y0 - w, w), -1: (y0, y1, w)}[dt]
        xs, xd, xn = {0: (XH, XH, cx), 1: (cx, 0, XH), -1: (XH, XH + cx, XH)}[dg]
        return (pl.ds(ys, yn), pl.ds(xs, xn)), (pl.ds(yd, yn), pl.ds(xd, xn))

    def halo(buf, w, slot, sides):
        copies = []
        for k, (dg, dt) in enumerate(sides):
            a, b = span(dg, dt, w)
            copies.append(pltpu.make_async_remote_copy(
                src_ref=buf.at[a], dst_ref=buf.at[b], send_sem=send_sem.at[slot, k], recv_sem=recv_sem.at[slot, k],
                device_id=(g + dg, t + dt), device_id_type=MESH))
        return copies

    def blank(buf, w, sides, value):
        for dg, dt in sides:
            _, b = span(dg, dt, w)

            @pl.when(jnp.logical_not(exists(-dg, -dt)))
            def _():
                buf[b] = jnp.full((b[0].size, b[1].size, cz), value, F32)

    def begin(copies, sides):
        for c, (dg, dt) in zip(copies, sides):
            pl.when(exists(dg, dt))(c.start)

    def landed(copies, sides):
        for c, (dg, dt) in zip(copies, sides):
            pl.when(exists(-dg, -dt))(c.wait_recv)

    def left(copies, sides):
        for c, (dg, dt) in zip(copies, sides):
            pl.when(exists(dg, dt))(c.wait_send)

    blank(half, PW, SIDES, FAR)
    blank(src, SW, SIDES, 0.0)
    blank(s2, 1, SIDES[:4], 0.0)
    kinds = [0.5 / jnp.full((1, cz), table[k], F32) for k in range(nf)]
    for c in loads_f:
        c.wait()

    def paint(y):
        f = raw_f[:, y, :]
        p = jnp.broadcast_to(kinds[0], (cx, cz))
        for k in range(1, nf):
            p = jnp.where(f == k, kinds[k], p)
        half[y0 + y, pl.ds(XH, cx), :] = p

    for y in range(cy):
        paint(y)
    pl.semaphore_wait(barrier, n - 1)
    half_out = halo(half, PW, 0, SIDES)
    src_out = halo(src, SW, 1, SIDES)
    begin(half_out, SIDES)
    for c in loads_s:
        c.wait()
    for y in range(cy):
        src[y0 + y, pl.ds(XH, cx), :] = raw_s[:, y, :]
    begin(src_out, SIDES)

    def xp(v):
        return pltpu.roll(v, ex - 1, 0)

    def xm(v):
        return pltpu.roll(v, 1, 0)

    def zp(v):
        return pltpu.roll(v, cz - 1, 1)

    def zm(v):
        return pltpu.roll(v, 1, 1)

    last_z = lax.broadcasted_iota(jnp.int32, (ex, cz), 1) == cz - 1
    own = pl.ds(XH, cx)

    def loop(lo, hi, body):
        def step(y, carry):
            body(y)
            return carry

        lax.fori_loop(lo, hi, step, 0, unroll=2)

    def side_faces(y):
        p = half[y]
        fx = recip(p + xp(p))
        fz = jnp.where(last_z, 0.0, recip(p + zp(p)))
        tx[y] = fx
        tz[y] = fz
        wt[y] = storage + (fx + xm(fx)) + (fz + zm(fz))

    def next_faces(y):
        ty[y] = recip(half[y] + half[y + 1])

    def first(y):
        w = RELAX * recip(wt[y] + ty[y] + ty[y - 1])
        wt[y] = w
        h1[y] = w * src[y]

    def sweep(v_ref, y):
        v = v_ref[y]
        fx, fz = tx[y], tz[y]
        total = src[y] + ty[y] * v_ref[y + 1] + ty[y - 1] * v_ref[y - 1]
        total = total + (fx * xp(v) + xm(fx * v)) + (fz * zp(v) + zm(fz * v))
        return (1.0 - RELAX) * v + wt[y] * total

    def second(y):
        h2[y] = sweep(h1, y)

    own_x = lax.broadcasted_iota(jnp.int32, (cx, cz), 0)

    def sweep_own(v_ref, y):
        v = v_ref[y, own, :]
        fx, fz = tx[y, own, :], tz[y, own, :]
        v_low, f_low = v_ref[y, pl.ds(XH - 1, 1), :], tx[y, pl.ds(XH - 1, 1), :]
        v_high = v_ref[y, pl.ds(XH + cx, 1), :]
        v_next = jnp.where(own_x == cx - 1, v_high, pltpu.roll(v, cx - 1, 0))
        back = jnp.where(own_x == 0, f_low * v_low, pltpu.roll(fx * v, 1, 0))
        total = src[y, own, :] + ty[y, own, :] * v_ref[y + 1, own, :] + ty[y - 1, own, :] * v_ref[y - 1, own, :]
        total = total + (fx * v_next + back) + (fz * zp(v) + zm(fz * v))
        return (1.0 - RELAX) * v + wt[y, own, :] * total

    landed(half_out[2:4], SIDES[2:4])
    loop(y0, y1, side_faces)
    loop(y0, y1 - 1, next_faces)
    landed(src_out[2:4], SIDES[2:4])
    loop(y0 + 1, y1 - 1, first)
    loop(y0 + 2, y1 - 2, second)

    def gather_sum(y, acc):
        inner = src[y, own, :] - storage * h2[y, own, :]
        return acc + jnp.sum(inner.reshape(cx // 8, 8, cz), axis=0)

    acc = lax.fori_loop(y0 + 2, y1 - 2, gather_sum, jnp.zeros((8, cz), F32), unroll=2)
    rest_sides = SIDES[:2] + SIDES[4:]
    landed(half_out[:2] + half_out[4:], rest_sides)
    loop(y0 - 2, y0, side_faces)
    loop(y1, y1 + 2, side_faces)
    loop(y0 - 3, y0, next_faces)
    loop(y1 - 1, y1 + 2, next_faces)
    landed(src_out[:2] + src_out[4:], rest_sides)
    loop(y0 - 2, y0 + 1, first)
    loop(y1 - 1, y1 + 2, first)
    loop(y0 - 1, y0 + 2, second)
    loop(y1 - 2, y1 + 1, second)

    for lo, hi in ((y0, y0 + 2), (y1 - 2, y1)):
        acc = lax.fori_loop(lo, hi, gather_sum, acc, unroll=2)
    edge = ty[y1 - 1, own, :] * (h2[y1 - 1, own, :] - h2[y1, own, :]) + ty[y0 - 1, own, :] * (h2[y0, own, :] - h2[y0 - 1, own, :])
    acc = acc - jnp.sum(edge.reshape(cx // 8, 8, cz), axis=0)
    rows = pl.ds(y0, cy)

    def x_face(x):
        a = tx[rows, pl.ds(x - 7, 8), :][:, 7, :]
        b = h2[rows, pl.ds(x - 7, 8), :][:, 7, :]
        c = h2[rows, pl.ds(x + 1, 8), :][:, 0, :]
        return a * (b - c)

    side = x_face(XH - 1) - x_face(XH + cx - 1)
    acc = acc + jnp.where(lax.broadcasted_iota(jnp.int32, (8, cz), 0) == 0, jnp.sum(side, axis=0, keepdims=True), 0.0)
    rhs = jnp.sum(jnp.sum(acc, axis=0, keepdims=True), axis=1, keepdims=True)
    link_x = jnp.sum(jnp.sum(tx[pl.ds(y0, cy), pl.ds(XH + cx - 8, 8), :][:, 7, :], axis=0, keepdims=True), axis=1, keepdims=True)
    link_y = jnp.sum(jnp.sum(ty[y1 - 1, own, :], axis=0, keepdims=True), axis=1, keepdims=True)
    lane = lax.broadcasted_iota(jnp.int32, (1, 128), 1)
    packed = jnp.where(lane == g, rhs, jnp.where(lane == g + 32, link_x, jnp.where(lane == g + 64, link_y, 0.0)))
    mine[...] = packed
    gath[me] = packed

    def to(other):
        return pltpu.make_async_remote_copy(
            src_ref=mine, dst_ref=gath.at[me], send_sem=cs_sem, recv_sem=cr_sem,
            device_id=(other // tiles, lax.rem(other, tiles)), device_id_type=MESH)

    def tell(k, carry):
        to(lax.rem(me + k, n)).start()
        return carry

    lax.fori_loop(1, n, tell, 0)
    rest = gath.at[pl.ds(0, n - 1)]

    def third(y):
        s2[y, own, :] = sweep_own(h2, y)

    four = SIDES[:4]
    s2_out = halo(s2, 1, 2, four)
    loop(y0, y0 + 1, third)
    pl.when(exists(0, -1))(s2_out[1].start)
    loop(y1 - 1, y1, third)
    pl.when(exists(0, 1))(s2_out[0].start)
    loop(y0 + 1, y1 - 1, third)
    begin(s2_out[2:], four[2:])
    pltpu.make_async_copy(rest, rest, cr_sem).wait()

    lanes = lax.broadcasted_iota(jnp.int32, (tiles, 128), 1)
    whole = jnp.sum(gath[...].reshape(groups, tiles, 128), axis=0)
    c_rhs = jnp.where(lanes < groups, whole, 0.0)
    c_lx = jnp.where(lanes < groups, pltpu.roll(whole, 96, 1), 0.0)
    c_ly = jnp.where(lanes < groups, pltpu.roll(whole, 64, 1), 0.0)

    def before(v, s):
        return pltpu.roll(v, s, 0)

    def after(v, s):
        return pltpu.roll(v, tiles - s, 0)

    lx_prev = pltpu.roll(c_lx, 1, 1)
    ly_prev = before(c_ly, 1)
    diag = storage * cx * cy * cz + c_lx + lx_prev + c_ly + ly_prev
    lower, upper = -ly_prev, -c_ly
    steps = []
    stride = 1
    while stride < tiles:
        alpha = -lower * recip(before(diag, stride))
        gamma = -upper * recip(after(diag, stride))
        steps.append((stride, alpha, gamma))
        diag = diag + alpha * before(upper, stride) + gamma * after(lower, stride)
        lower, upper = alpha * before(lower, stride), gamma * after(upper, stride)
        stride *= 2
    inv = recip(diag)
    corr = None
    for _ in range(COARSE_ITERS):
        r = c_rhs
        if corr is not None:
            r = r + lx_prev * pltpu.roll(corr, 1, 1) + c_lx * pltpu.roll(corr, 127, 1)
        for stride, alpha, gamma in steps:
            r = r + alpha * before(r, stride) + gamma * after(r, stride)
        corr = r * inv

    row_t = lax.broadcasted_iota(jnp.int32, (tiles, 128), 0)

    def pick(dg, dt):
        hit = jnp.logical_and(row_t == t + dt, lanes == g + dg)
        one = jnp.sum(jnp.where(hit, corr, 0.0), axis=0, keepdims=True)
        return jnp.broadcast_to(jnp.sum(one, axis=1, keepdims=True), (1, cz))

    cols = [[pick(dg, dt) for dg in (-1, 0, 1)] for dt in (-1, 0, 1)]
    xrow = lax.broadcasted_iota(jnp.int32, (ex, cz), 0)

    def spread(line, ahead):
        return jnp.where(xrow < XH - ahead, line[0], jnp.where(xrow < XH + cx - ahead, line[1], line[2]))

    c_low, c_mid, c_high = [spread(line, 0) for line in cols]
    landed(s2_out, four)

    def lift(y, c, line, extra):
        across = tx[y] * (spread(line, 1) - c)
        h4[y] = s2[y] + c + wt[y] * (across - xm(across) - storage * c + extra)

    loop(y0 + 1, y1 - 1, lambda y: lift(y, c_mid, cols[1], 0.0))
    lift(y0 - 1, c_low, cols[0], ty[y0 - 1] * (c_mid - c_low))
    lift(y0, c_mid, cols[1], ty[y0 - 1] * (c_low - c_mid))
    lift(y1 - 1, c_mid, cols[1], ty[y1 - 1] * (c_high - c_mid))
    lift(y1, c_high, cols[2], ty[y1 - 1] * (c_mid - c_high))

    def store(k):
        return pltpu.make_async_copy(res.at[k], out.at[:, k, :], out_sem.at[k])

    for k in range(cy):
        res[k] = sweep_own(h4, y0 + k)
        store(k).start()
    left(half_out, SIDES)
    left(src_out, SIDES)
    left(s2_out, four)
    pltpu.make_async_copy(rest, rest, cs_sem).wait()
    for k in range(cy):
        store(k).wait()


def solution(mesh):
    groups, tiles = mesh.shape["group"], mesh.shape["tile"]

    def on_device(facies, table, source):
        cx, cy, cz = source.shape
        ext = pltpu.VMEM((cy + 2 * PW, cx + 2 * XH, cz), F32)
        n = groups * tiles
        return pl.pallas_call(
            functools.partial(kernel, groups, tiles),
            out_shape=jax.ShapeDtypeStruct(source.shape, F32),
            in_specs=[pl.BlockSpec(memory_space=pl.ANY), pl.BlockSpec(memory_space=pltpu.SMEM), pl.BlockSpec(memory_space=pl.ANY)],
            out_specs=pl.BlockSpec(memory_space=pl.ANY),
            scratch_shapes=[
                pltpu.VMEM((cx, cy, cz), jnp.int32),
                pltpu.VMEM((cx, cy, cz), F32),
                ext, ext, ext, ext, ext, ext, ext, ext, ext, ext,
                pltpu.VMEM((cy, cx, cz), F32),
                pltpu.VMEM((1, 128), F32),
                pltpu.VMEM((n, 1, 128), F32),
                pltpu.SemaphoreType.DMA((8,)),
                pltpu.SemaphoreType.DMA((cy,)),
                pltpu.SemaphoreType.DMA((3, 8)),
                pltpu.SemaphoreType.DMA((3, 8)),
                pltpu.SemaphoreType.DMA,
                pltpu.SemaphoreType.DMA,
            ],
            compiler_params=pltpu.CompilerParams(
                collective_id=0, has_side_effects=True, vmem_limit_bytes=53 * 1024 * 1024),
        )(facies, table, source)

    placed = (P("group", "tile", None), P(), P("group", "tile", None))
    return jax.shard_map(on_device, mesh=mesh, in_specs=placed, out_specs=P("group", "tile", None), check_vma=False)
```

```python
import functools

import jax
import jax.numpy as jnp
from jax import lax
from jax.experimental import pallas as pl
from jax.experimental.pallas import tpu as pltpu
from jax.sharding import PartitionSpec as P

COARSE_ITERS = 3
RELAX = 0.8
MESH = pl.DeviceIdType.MESH
F32 = jnp.float32

PW = 3
SW = 2
XH = 8
SIDES = [(0, 1), (0, -1), (1, 0), (-1, 0), (1, 1), (1, -1), (-1, 1), (-1, -1)]


FAR = 1e36


def recip(x):
    y = pl.reciprocal(x, approx=True)
    return y * (2.0 - x * y)


def kernel(groups, tiles, facies, table, source, out, raw_f, raw_s, half, src, tx, ty, tz, wt, h1, h2, h4, s2, res,
           mine, gath, in_sem, out_sem, send_sem, recv_sem, cs_sem, cr_sem):
    cx, cy, cz = source.shape
    nf = table.shape[0]
    n = groups * tiles
    g = lax.axis_index("group")
    t = lax.axis_index("tile")
    me = g * tiles + t
    ex = cx + 2 * XH
    y0, y1 = PW, PW + cy
    storage = 0.01 / cy

    barrier = pltpu.get_barrier_semaphore()

    def greet(k, carry):
        other = lax.rem(me + k, n)
        pl.semaphore_signal(barrier, inc=1, device_id=(other // tiles, lax.rem(other, tiles)), device_id_type=MESH)
        return carry

    lax.fori_loop(1, n, greet, 0)

    piece = cx // 4
    loads_f = [pltpu.make_async_copy(facies.at[pl.ds(k * piece, piece)], raw_f.at[pl.ds(k * piece, piece)], in_sem.at[k]) for k in range(4)]
    loads_s = [pltpu.make_async_copy(source.at[pl.ds(k * piece, piece)], raw_s.at[pl.ds(k * piece, piece)], in_sem.at[4 + k]) for k in range(4)]
    for c in loads_s + loads_f:
        c.start()

    def exists(dg, dt):
        ok = None
        for pos, d, count in ((g, dg, groups), (t, dt, tiles)):
            if d:
                one = pos < count - 1 if d > 0 else pos > 0
                ok = one if ok is None else jnp.logical_and(ok, one)
        return ok

    def span(dg, dt, w):
        ys, yd, yn = {0: (y0, y0, cy), 1: (y1 - w, y0 - w, w), -1: (y0, y1, w)}[dt]
        xs, xd, xn = {0: (XH, XH, cx), 1: (cx, 0, XH), -1: (XH, XH + cx, XH)}[dg]
        return (pl.ds(ys, yn), pl.ds(xs, xn)), (pl.ds(yd, yn), pl.ds(xd, xn))

    def halo(buf, w, slot, sides):
        copies = []
        for k, (dg, dt) in enumerate(sides):
            a, b = span(dg, dt, w)
            copies.append(pltpu.make_async_remote_copy(
                src_ref=buf.at[a], dst_ref=buf.at[b], send_sem=send_sem.at[slot, k], recv_sem=recv_sem.at[slot, k],
                device_id=(g + dg, t + dt), device_id_type=MESH))
        return copies

    def blank(buf, w, sides, value):
        for dg, dt in sides:
            _, b = span(dg, dt, w)

            @pl.when(jnp.logical_not(exists(-dg, -dt)))
            def _():
                buf[b] = jnp.full((b[0].size, b[1].size, cz), value, F32)

    def begin(copies, sides):
        for c, (dg, dt) in zip(copies, sides):
            pl.when(exists(dg, dt))(c.start)

    def landed(copies, sides):
        for c, (dg, dt) in zip(copies, sides):
            pl.when(exists(-dg, -dt))(c.wait_recv)

    def left(copies, sides):
        for c, (dg, dt) in zip(copies, sides):
            pl.when(exists(dg, dt))(c.wait_send)

    blank(half, PW, SIDES, FAR)
    blank(src, SW, SIDES, 0.0)
    blank(s2, 1, SIDES[:4], 0.0)
    for c in loads_s:
        c.wait()
    for y in range(cy):
        src[y0 + y, pl.ds(XH, cx), :] = raw_s[:, y, :]
    pl.semaphore_wait(barrier, n - 1)
    half_out = halo(half, PW, 0, SIDES)
    src_out = halo(src, SW, 1, SIDES)
    begin(src_out, SIDES)
    kinds = [0.5 / jnp.full((1, cz), table[k], F32) for k in range(nf)]
    for c in loads_f:
        c.wait()

    def paint(y):
        f = raw_f[:, y, :]
        p = jnp.broadcast_to(kinds[0], (cx, cz))
        for k in range(1, nf):
            p = jnp.where(f == k, kinds[k], p)
        half[y0 + y, pl.ds(XH, cx), :] = p

    for y in range(cy):
        paint(y)
    begin(half_out, SIDES)

    def xp(v):
        return pltpu.roll(v, ex - 1, 0)

    def xm(v):
        return pltpu.roll(v, 1, 0)

    def zp(v):
        return pltpu.roll(v, cz - 1, 1)

    def zm(v):
        return pltpu.roll(v, 1, 1)

    last_z = lax.broadcasted_iota(jnp.int32, (ex, cz), 1) == cz - 1
    own = pl.ds(XH, cx)

    def loop(lo, hi, body):
        def step(y, carry):
            body(y)
            return carry

        lax.fori_loop(lo, hi, step, 0, unroll=2)

    def side_faces(y):
        p = half[y]
        fx = recip(p + xp(p))
        fz = jnp.where(last_z, 0.0, recip(p + zp(p)))
        tx[y] = fx
        tz[y] = fz
        wt[y] = storage + (fx + xm(fx)) + (fz + zm(fz))

    def next_faces(y):
        ty[y] = recip(half[y] + half[y + 1])

    def first(y):
        w = RELAX * recip(wt[y] + ty[y] + ty[y - 1])
        wt[y] = w
        h1[y] = w * src[y]

    def sweep(v_ref, y):
        v = v_ref[y]
        fx, fz = tx[y], tz[y]
        total = src[y] + ty[y] * v_ref[y + 1] + ty[y - 1] * v_ref[y - 1]
        total = total + (fx * xp(v) + xm(fx * v)) + (fz * zp(v) + zm(fz * v))
        return (1.0 - RELAX) * v + wt[y] * total

    def second(y):
        h2[y] = sweep(h1, y)

    own_x = lax.broadcasted_iota(jnp.int32, (cx, cz), 0)

    def sweep_own(v_ref, y):
        v = v_ref[y, own, :]
        fx, fz = tx[y, own, :], tz[y, own, :]
        v_low, f_low = v_ref[y, pl.ds(XH - 1, 1), :], tx[y, pl.ds(XH - 1, 1), :]
        v_high = v_ref[y, pl.ds(XH + cx, 1), :]
        v_next = jnp.where(own_x == cx - 1, v_high, pltpu.roll(v, cx - 1, 0))
        back = jnp.where(own_x == 0, f_low * v_low, pltpu.roll(fx * v, 1, 0))
        total = src[y, own, :] + ty[y, own, :] * v_ref[y + 1, own, :] + ty[y - 1, own, :] * v_ref[y - 1, own, :]
        total = total + (fx * v_next + back) + (fz * zp(v) + zm(fz * v))
        return (1.0 - RELAX) * v + wt[y, own, :] * total

    landed(half_out[2:4], SIDES[2:4])
    loop(y0, y1, side_faces)
    loop(y0, y1 - 1, next_faces)
    landed(src_out[2:4], SIDES[2:4])
    loop(y0 + 1, y1 - 1, first)
    loop(y0 + 2, y1 - 2, second)

    def gather_sum(y, acc):
        inner = src[y, own, :] - storage * h2[y, own, :]
        return acc + jnp.sum(inner.reshape(cx // 8, 8, cz), axis=0)

    acc = lax.fori_loop(y0 + 2, y1 - 2, gather_sum, jnp.zeros((8, cz), F32), unroll=2)
    rest_sides = SIDES[:2] + SIDES[4:]
    landed(half_out[:2] + half_out[4:], rest_sides)
    loop(y0 - 2, y0, side_faces)
    loop(y1, y1 + 2, side_faces)
    loop(y0 - 3, y0, next_faces)
    loop(y1 - 1, y1 + 2, next_faces)
    landed(src_out[:2] + src_out[4:], rest_sides)
    loop(y0 - 2, y0 + 1, first)
    loop(y1 - 1, y1 + 2, first)
    loop(y0 - 1, y0 + 2, second)
    loop(y1 - 2, y1 + 1, second)

    for lo, hi in ((y0, y0 + 2), (y1 - 2, y1)):
        acc = lax.fori_loop(lo, hi, gather_sum, acc, unroll=2)
    edge = ty[y1 - 1, own, :] * (h2[y1 - 1, own, :] - h2[y1, own, :]) + ty[y0 - 1, own, :] * (h2[y0, own, :] - h2[y0 - 1, own, :])
    acc = acc - jnp.sum(edge.reshape(cx // 8, 8, cz), axis=0)
    rows = pl.ds(y0, cy)

    def x_face(x):
        a = tx[rows, pl.ds(x - 7, 8), :][:, 7, :]
        b = h2[rows, pl.ds(x - 7, 8), :][:, 7, :]
        c = h2[rows, pl.ds(x + 1, 8), :][:, 0, :]
        return a * (b - c)

    side = x_face(XH - 1) - x_face(XH + cx - 1)
    acc = acc + jnp.where(lax.broadcasted_iota(jnp.int32, (8, cz), 0) == 0, jnp.sum(side, axis=0, keepdims=True), 0.0)
    rhs = jnp.sum(jnp.sum(acc, axis=0, keepdims=True), axis=1, keepdims=True)
    link_x = jnp.sum(jnp.sum(tx[pl.ds(y0, cy), pl.ds(XH + cx - 8, 8), :][:, 7, :], axis=0, keepdims=True), axis=1, keepdims=True)
    link_y = jnp.sum(jnp.sum(ty[y1 - 1, own, :], axis=0, keepdims=True), axis=1, keepdims=True)
    lane = lax.broadcasted_iota(jnp.int32, (1, 128), 1)
    packed = jnp.where(lane == g, rhs, jnp.where(lane == g + 32, link_x, jnp.where(lane == g + 64, link_y, 0.0)))
    mine[...] = packed
    gath[me] = packed

    def to(other):
        return pltpu.make_async_remote_copy(
            src_ref=mine, dst_ref=gath.at[me], send_sem=cs_sem, recv_sem=cr_sem,
            device_id=(other // tiles, lax.rem(other, tiles)), device_id_type=MESH)

    def tell(k, carry):
        to(lax.rem(me + k, n)).start()
        return carry

    lax.fori_loop(1, n, tell, 0)
    rest = gath.at[pl.ds(0, n - 1)]

    def third(y):
        s2[y, own, :] = sweep_own(h2, y)

    four = SIDES[:4]
    s2_out = halo(s2, 1, 2, four)
    loop(y0, y0 + 1, third)
    pl.when(exists(0, -1))(s2_out[1].start)
    loop(y1 - 1, y1, third)
    pl.when(exists(0, 1))(s2_out[0].start)
    loop(y0 + 1, y1 - 1, third)
    begin(s2_out[2:], four[2:])
    pltpu.make_async_copy(rest, rest, cr_sem).wait()

    lanes = lax.broadcasted_iota(jnp.int32, (tiles, 128), 1)
    whole = jnp.sum(gath[...].reshape(groups, tiles, 128), axis=0)
    c_rhs = jnp.where(lanes < groups, whole, 0.0)
    c_lx = jnp.where(lanes < groups, pltpu.roll(whole, 96, 1), 0.0)
    c_ly = jnp.where(lanes < groups, pltpu.roll(whole, 64, 1), 0.0)

    def before(v, s):
        return pltpu.roll(v, s, 0)

    def after(v, s):
        return pltpu.roll(v, tiles - s, 0)

    lx_prev = pltpu.roll(c_lx, 1, 1)
    ly_prev = before(c_ly, 1)
    diag = storage * cx * cy * cz + c_lx + lx_prev + c_ly + ly_prev
    lower, upper = -ly_prev, -c_ly
    steps = []
    stride = 1
    while stride < tiles:
        alpha = -lower * recip(before(diag, stride))
        gamma = -upper * recip(after(diag, stride))
        steps.append((stride, alpha, gamma))
        diag = diag + alpha * before(upper, stride) + gamma * after(lower, stride)
        lower, upper = alpha * before(lower, stride), gamma * after(upper, stride)
        stride *= 2
    inv = recip(diag)
    corr = None
    for _ in range(COARSE_ITERS):
        r = c_rhs
        if corr is not None:
            r = r + lx_prev * pltpu.roll(corr, 1, 1) + c_lx * pltpu.roll(corr, 127, 1)
        for stride, alpha, gamma in steps:
            r = r + alpha * before(r, stride) + gamma * after(r, stride)
        corr = r * inv

    row_t = lax.broadcasted_iota(jnp.int32, (tiles, 128), 0)

    def pick(dg, dt):
        hit = jnp.logical_and(row_t == t + dt, lanes == g + dg)
        one = jnp.sum(jnp.where(hit, corr, 0.0), axis=0, keepdims=True)
        return jnp.broadcast_to(jnp.sum(one, axis=1, keepdims=True), (1, cz))

    cols = [[pick(dg, dt) for dg in (-1, 0, 1)] for dt in (-1, 0, 1)]
    xrow = lax.broadcasted_iota(jnp.int32, (ex, cz), 0)

    def spread(line, ahead):
        return jnp.where(xrow < XH - ahead, line[0], jnp.where(xrow < XH + cx - ahead, line[1], line[2]))

    c_low, c_mid, c_high = [spread(line, 0) for line in cols]
    landed(s2_out, four)

    def lift(y, c, line, extra):
        across = tx[y] * (spread(line, 1) - c)
        h4[y] = s2[y] + c + wt[y] * (across - xm(across) - storage * c + extra)

    loop(y0 + 1, y1 - 1, lambda y: lift(y, c_mid, cols[1], 0.0))
    lift(y0 - 1, c_low, cols[0], ty[y0 - 1] * (c_mid - c_low))
    lift(y0, c_mid, cols[1], ty[y0 - 1] * (c_low - c_mid))
    lift(y1 - 1, c_mid, cols[1], ty[y1 - 1] * (c_high - c_mid))
    lift(y1, c_high, cols[2], ty[y1 - 1] * (c_mid - c_high))

    def store(k):
        return pltpu.make_async_copy(res.at[k], out.at[:, k, :], out_sem.at[k])

    for k in range(cy):
        res[k] = sweep_own(h4, y0 + k)
        store(k).start()
    left(half_out, SIDES)
    left(src_out, SIDES)
    left(s2_out, four)
    pltpu.make_async_copy(rest, rest, cs_sem).wait()
    for k in range(cy):
        store(k).wait()


def solution(mesh):
    groups, tiles = mesh.shape["group"], mesh.shape["tile"]

    def on_device(facies, table, source):
        cx, cy, cz = source.shape
        ext = pltpu.VMEM((cy + 2 * PW, cx + 2 * XH, cz), F32)
        n = groups * tiles
        return pl.pallas_call(
            functools.partial(kernel, groups, tiles),
            out_shape=jax.ShapeDtypeStruct(source.shape, F32),
            in_specs=[pl.BlockSpec(memory_space=pl.ANY), pl.BlockSpec(memory_space=pltpu.SMEM), pl.BlockSpec(memory_space=pl.ANY)],
            out_specs=pl.BlockSpec(memory_space=pl.ANY),
            scratch_shapes=[
                pltpu.VMEM((cx, cy, cz), jnp.int32),
                pltpu.VMEM((cx, cy, cz), F32),
                ext, ext, ext, ext, ext, ext, ext, ext, ext, ext,
                pltpu.VMEM((cy, cx, cz), F32),
                pltpu.VMEM((1, 128), F32),
                pltpu.VMEM((n, 1, 128), F32),
                pltpu.SemaphoreType.DMA((8,)),
                pltpu.SemaphoreType.DMA((cy,)),
                pltpu.SemaphoreType.DMA((3, 8)),
                pltpu.SemaphoreType.DMA((3, 8)),
                pltpu.SemaphoreType.DMA,
                pltpu.SemaphoreType.DMA,
            ],
            compiler_params=pltpu.CompilerParams(
                collective_id=0, has_side_effects=True, vmem_limit_bytes=53 * 1024 * 1024),
        )(facies, table, source)

    placed = (P("group", "tile", None), P(), P("group", "tile", None))
    return jax.shard_map(on_device, mesh=mesh, in_specs=placed, out_specs=P("group", "tile", None), check_vma=False)
```
